512 devices in a mesh: turn: 128 (over y, x, z_lo), hand: 4 (over z_hi, core).
Axes of the slice: x: 4, y: 4, z: 16 (z_hi: 2, z_lo: 8; z = z_hi * 8 + z_lo), core: 2. Of those that a mesh axis runs over, the one named last changes fastest.
Arguments:
- reach: bfloat16 [512, 81, 1024], P('turn', None, 'hand'), may hold values from 0.019897461 to 1
- ranks: int32 [512, 1024], P('turn', 'hand'), may hold values from 0 to 7461
- live: int32 [512, 1024], P('turn', 'hand'), may hold values 0 or 1
- turn_of: int32 [512], P('turn'), may hold values from 0 to 48, never falling along the last dimension, each value on 1 to 48 neighbouring positions
- hand_cards: int32 [2, 1024], replicated, may hold values from 0 to 51, as said below
- pot: float32 [81], replicated, may hold values from 1 to 8
- turn_act: int32 [81], replicated, may hold values from 0 to 8
- flop_act: int32 [81], replicated, may hold values from 0 to 8
- turn_regret: float32 [49, 9, 1024], P(None, None, 'hand'), may hold values from 0.1 to 10
- flop_regret: float32 [9, 1024], P(None, 'hand'), may hold values from 0.05 to 5
Outputs:
- new_turn_regret: float32 [49, 9, 1024], P(None, None, 'hand')
- new_flop_regret: float32 [9, 1024], P(None, 'hand')
- turn_values: float32 [49, 1024], P(None, 'hand')
The draws below stay inside these ranges and needn't reach their ends.
Inputs may be any that keep to these rules, and one draw needn't show every extreme that they name: `hand_cards`: each column holds two different cards of a 52-card deck, and no two hands are alike. `turn_of`: the boards of one turn card stand in a row, in rising order of turn card, at most 48 boards a turn card.
All inputs are finite; a program needn't handle non-finite values. No bound on the sum of `live` on one device may be relied on, other than what follows from the above.
Results may differ from the reference program's by a relative error of at most 0.0003.
Values may be sent and summed in bfloat16 or wider, within the bound.
No kernel may reach another device: no remote copies, remote signals or barrier semaphores. Data moves between devices by JAX's collectives and lax.ppermute only.
A program may use at most 64 MiB of HBM per device.

```python
import math
import jax
import jax.numpy as jnp
import numpy as np
from jax import lax

H = 1024
S = 81
TURNS = 49
RIVERS = 48
A = 9
F = 9
BOARDS = 512


def draw_hand_cards(key, part):
    key = jax.random.fold_in(key, 11)
    table = jnp.asarray(np.array([[a, b] for a in range(52) for b in range(a + 1, 52)], np.int32))
    order = jax.random.permutation(key, 1326)[:H]
    return jnp.take(table, order, axis=0).T.astype(jnp.int32)


def place_ends(result, rng, least, high):
    extent = result.shape
    index_at = [jax.random.randint(jax.random.fold_in(rng, axis), (), 0, extent[axis]) for axis in range(len(extent))]
    result = result.at[tuple(index_at)].set(least)
    longest = extent.index(max(extent))
    index_at[longest] = (index_at[longest] + 1) % extent[longest]
    return result.at[tuple(index_at)].set(high)


def shard_levels(stream_key, dims, cuts, least, largest):
    gain = 1.0
    for axis_at, shards_of in cuts:
        steps = jax.random.uniform(jax.random.fold_in(jax.random.fold_in(stream_key, 6), axis_at), (shards_of,), jnp.float32, least / len(cuts), largest / len(cuts))
        gain = gain * jnp.repeat(jnp.exp(steps), dims[axis_at] // shards_of).reshape((-1,) + (1,) * (len(dims) - 1 - axis_at))
    return gain


def profile(count, total, most, lean):
    portions = [(1 << 20) // math.isqrt(grade ** lean) + 1 for grade in range(2, count + 1)]
    rest, holding = total - most - (count - 1), [1] * (count - 1)
    while rest > 0:
        movable = [i for i in range(count - 1) if holding[i] < most]
        mass, left = sum([portions[i] for i in movable]), rest
        for i in movable:
            addition = min(most - holding[i], max(1, left * portions[i] // mass), rest)
            holding[i] = holding[i] + addition
            rest = rest - addition
    return np.array([most] + holding)


def uneven(stream_key, number_of, total, bound, slope):
    if number_of == 2:
        one = jax.random.randint(stream_key, (), max(1, total - bound), min(bound, total - 1) + 1)
        return jnp.stack([one, total - one])
    lengths = jnp.asarray(profile(number_of, total, bound, slope), jnp.int32)
    twos = (number_of - 1) // 2
    donor, sink = lengths[1:1 + 2 * twos:2], lengths[2:2 + 2 * twos:2]
    slack = jnp.minimum(donor - 1, bound - sink)
    moved = jax.random.randint(jax.random.fold_in(stream_key, 1), (twos,), 0, 1 << 20) % (slack + 1)
    lengths = lengths.at[1:1 + 2 * twos:2].set(donor - moved).at[2:2 + 2 * twos:2].set(sink + moved)
    return lengths[jax.random.permutation(jax.random.fold_in(stream_key, 2), number_of)]


def setup_inputs(seed: int = 0) -> dict:
    splits = jax.random.split(jax.random.key(seed), 11)
    reach = jnp.clip(jnp.exp(math.log(1.0) - 3.9171631 * jax.random.uniform(splits[0], (BOARDS, S, H), jnp.float32) ** shard_levels(splits[0], (BOARDS, S, H), ((0, 128), (2, 4)), -0.2, 0.2)), 0.019897461, 1.0).astype(jnp.bfloat16)
    ranks = place_ends(jax.random.randint(splits[1], (BOARDS, H), 0, 7462), jax.random.fold_in(splits[1], 1), 0, 7461).astype(jnp.int32)
    live = place_ends((jax.random.randint(splits[2], (BOARDS, H), 0, 8) < 7).astype(jnp.int32), jax.random.fold_in(splits[2], 1), 0, 1)
    turn_of = jnp.searchsorted(jnp.cumsum(uneven(splits[3], TURNS, BOARDS, RIVERS, 1)), jnp.arange(BOARDS), side="right").astype(jnp.int32)
    hand_cards = draw_hand_cards(jax.random.fold_in(splits[10], 71), 0)
    pot = jnp.clip(jnp.exp(jax.random.uniform(splits[5], (S,), jnp.float32, math.log(1.0), math.log(8.0))), 1.0, 8.0)
    turn_act = place_ends(jax.random.randint(splits[6], (S,), 0, A), jax.random.fold_in(splits[6], 1), 0, A - 1).astype(jnp.int32)
    flop_act = place_ends(jax.random.randint(splits[7], (S,), 0, F), jax.random.fold_in(splits[7], 1), 0, F - 1).astype(jnp.int32)
    turn_regret = jnp.clip(jnp.exp(math.log(10.0) - 4.6051702 * jax.random.uniform(splits[8], (TURNS, A, H), jnp.float32) ** shard_levels(splits[8], (TURNS, A, H), ((2, 4),), -0.2, 0.2)), 0.1, 10.0)
    flop_regret = jnp.clip(jnp.exp(math.log(5.0) - 4.6051702 * jax.random.uniform(splits[9], (F, H), jnp.float32) ** shard_levels(splits[9], (F, H), ((1, 4),), -0.2, 0.2)), 0.05, 5.0)
    return dict(reach=reach, ranks=ranks, live=live, turn_of=turn_of, hand_cards=hand_cards, pot=pot, turn_act=turn_act, flop_act=flop_act, turn_regret=turn_regret, flop_regret=flop_regret)


def reference(reach, ranks, live, turn_of, hand_cards, pot, turn_act, flop_act, turn_regret, flop_regret):
    first = hand_cards[0]
    second = hand_cards[1]
    apart = ((first[:, None] != first[None, :]) & (first[:, None] != second[None, :])
             & (second[:, None] != first[None, :]) & (second[:, None] != second[None, :])).astype(jnp.int32)
    scale = pot[:, None] / H

    def step(total, items):
        rows, rank_row, live_row, turn_id = items
        tile = (jnp.sign(rank_row[:, None] - rank_row[None, :]) * live_row[:, None] * live_row[None, :] * apart).astype(jnp.bfloat16)
        board_values = jnp.dot(rows, tile.T, preferred_element_type=jnp.float32) * scale
        return total.at[turn_id].add(board_values), None

    start = jnp.zeros((TURNS, S, H), jnp.float32)
    seq_values, unused = lax.scan(step, start, (reach, ranks, live, turn_of))
    turn_map = (turn_act[None, :] == jnp.arange(A, dtype=jnp.int32)[:, None]).astype(jnp.float32)
    flop_map = (flop_act[None, :] == jnp.arange(F, dtype=jnp.int32)[:, None]).astype(jnp.float32)
    q_turn = jnp.einsum("as,tsi->tai", turn_map, seq_values, precision=lax.Precision.HIGHEST) * (TURNS / BOARDS)
    flop_q = jnp.einsum("fs,si->fi", flop_map, jnp.sum(seq_values, axis=0), precision=lax.Precision.HIGHEST) / BOARDS
    turn_values = jnp.sum(turn_regret * q_turn, axis=1) / jnp.sum(turn_regret, axis=1)
    new_turn_regret = jnp.maximum(turn_regret + q_turn - turn_values[:, None, :], 0.0)
    flop_value = jnp.sum(flop_regret * flop_q, axis=0) / jnp.sum(flop_regret, axis=0)
    new_flop_regret = jnp.maximum(flop_regret + flop_q - flop_value[None, :], 0.0)
    return new_turn_regret, new_flop_regret, turn_values
```

```python
import jax
import jax.numpy as jnp
from jax import lax
from jax.experimental import pallas as pl
from jax.experimental.pallas import tpu as pltpu
from jax.sharding import PartitionSpec as P

SLOTS = 56
UNITS = 128
PLANE = 16
LINE = 8
VMEM = 48 * 1024 * 1024


def spread(count):
    return [pl.BlockSpec(memory_space=pltpu.VMEM)] * count


def scalars(count):
    return [pl.BlockSpec(memory_space=pltpu.SMEM)] * count


def weigh(pot, turn_act, flop_act, reach, ranks, live, out, acc):
    seqs, boards, width = reach.shape
    acc[...] = jnp.zeros_like(acc)
    half = acc.shape[0] // 2
    for s in range(seqs):
        term = reach[s].astype(jnp.float32) * pot[s]
        acc[turn_act[s]] += term
        acc[half + flop_act[s]] += term
    alive = live[...].astype(jnp.float32)
    for r in range(acc.shape[0]):
        out[pl.ds(r * boards, boards), :] = acc[r] * alive
    top = acc.shape[0] * boards
    out[pl.ds(top, boards), :] = ranks[...].astype(jnp.float32)
    out[pl.ds(top + boards, boards), :] = jnp.zeros((boards, width), jnp.float32)


def showdown(turn_of, payload, ranks, live, cards, out, acc):
    hands, rows, width = payload.shape
    boards = ranks.shape[0]
    actions = acc.shape[0] // (2 * boards)
    me = lax.axis_index("hand")
    used = acc.shape[0]
    here = cards[:, pl.ds(pl.multiple_of(me * width, width), width)].astype(jnp.float32)
    mine = jnp.concatenate(
        [ranks[...].astype(jnp.float32), here, jnp.zeros((2, width), jnp.float32)], axis=0
    )
    columns = jnp.transpose(mine)
    first, second = columns[:, boards : boards + 1], columns[:, boards + 1 : boards + 2]
    row = lax.broadcasted_iota(jnp.int32, (used, 1), 0) % boards
    total = jnp.zeros((used, width), jnp.float32)
    parts = [jnp.zeros((used, width), jnp.float32) for _ in range(boards)]
    for h in range(hands):
        x = payload[h, :used, :]
        high = x.astype(jnp.bfloat16)
        rest = x - high.astype(jnp.float32)
        mid = rest.astype(jnp.bfloat16)
        low = (rest - mid.astype(jnp.float32)).astype(jnp.bfloat16)
        there = cards[:, h * width : (h + 1) * width].astype(jnp.float32)
        one, two = there[0:1], there[1:2]
        shared = (first == one) | (first == two) | (second == one) | (second == two)
        apart = jnp.where(shared, 0.0, 1.0)
        for b in range(boards):
            theirs = payload[h, used + b : used + b + 1, :]
            sign = jnp.clip(columns[:, b : b + 1] - theirs, -1.0, 1.0)
            tile = (sign * apart).astype(jnp.bfloat16)
            for piece in (low, mid, high):
                parts[b] += lax.dot_general(
                    piece, tile, (((1,), (1,)), ((), ())), preferred_element_type=jnp.float32
                )
    for b in range(boards):
        alive = live[b : b + 1, :].astype(jnp.float32)
        total += jnp.where(row == b, parts[b], 0.0) * alive
    acc[...] = total
    slot = lax.broadcasted_iota(jnp.int32, (SLOTS, 128), 0)
    turns = 49
    hits = [(slot == turn_of[b]).astype(jnp.float32) for b in range(boards)]
    flop = (slot == turns).astype(jnp.float32)
    for a in range(actions):
        for half in range(width // 128):
            lanes = pl.ds(half * 128, 128)
            block = jnp.zeros((SLOTS, 128), jnp.float32)
            ends = jnp.zeros((1, 128), jnp.float32)
            for b in range(boards):
                block += hits[b] * acc[a * boards + b : a * boards + b + 1, lanes]
                at = (actions + a) * boards + b
                ends += acc[at : at + 1, lanes]
            block += flop * ends
            out[pl.ds((a * (width // 128) + half) * SLOTS, SLOTS), :] = block
    filled = actions * (width // 128) * SLOTS
    out[pl.ds(filled, UNITS * 8 - filled), :] = jnp.zeros((UNITS * 8 - filled, 128), jnp.float32)


def add_up(blocks, out):
    total = blocks[0]
    for k in range(1, blocks.shape[0]):
        total += blocks[k]
    for k in range(out.shape[0]):
        out[k] = total


def settle(turns_over_boards, over_boards, sums, turn_regret, flop_regret, turn_out, flop_out, values):
    actions, turns, width = turn_regret.shape
    halves = width // 128
    for half in range(halves):
        lanes = pl.ds(half * 128, 128)
        weighted = jnp.zeros((turns, 128), jnp.float32)
        weight = jnp.zeros((turns, 128), jnp.float32)
        top = jnp.zeros((1, 128), jnp.float32)
        bottom = jnp.zeros((1, 128), jnp.float32)
        for a in range(actions):
            base = (a * halves + half) * SLOTS
            regret = turn_regret[a, :, lanes]
            weighted += regret * (sums[pl.ds(base, turns), :] * turns_over_boards)
            weight += regret
            early = flop_regret[a : a + 1, lanes]
            top += early * (sums[pl.ds(base + turns, 1), :] * over_boards)
            bottom += early
        value = weighted / weight
        values[:, lanes] = value
        root = top / bottom
        for a in range(actions):
            base = (a * halves + half) * SLOTS
            q = sums[pl.ds(base, turns), :] * turns_over_boards
            turn_out[a, :, lanes] = jnp.maximum(turn_regret[a, :, lanes] + q - value, 0.0)
            q = sums[pl.ds(base + turns, 1), :] * over_boards
            flop_out[a : a + 1, lanes] = jnp.maximum(flop_regret[a : a + 1, lanes] + q - root, 0.0)


def shards(
    reach, ranks, live, turn_of, hand_cards, pot, turn_act, flop_act, turn_regret, flop_regret
):
    boards, _, width = reach.shape
    total_hands = hand_cards.shape[1]
    turns, actions, _ = turn_regret.shape
    rows = 2 * actions * boards
    boards_all = boards * lax.axis_size("turn")
    params = pltpu.CompilerParams(vmem_limit_bytes=VMEM)
    f32 = jnp.float32

    payload = pl.pallas_call(
        weigh,
        out_shape=jax.ShapeDtypeStruct((rows + 2 * boards, width), f32),
        in_specs=scalars(3) + spread(3),
        out_specs=pl.BlockSpec(memory_space=pltpu.VMEM),
        scratch_shapes=[pltpu.VMEM((2 * actions, boards, width), f32)],
        compiler_params=params,
    )(pot, turn_act, flop_act, jnp.transpose(reach, (1, 0, 2)), ranks, live)

    gathered = lax.all_gather(payload, "hand", axis=0, tiled=False)

    sums = pl.pallas_call(
        showdown,
        out_shape=jax.ShapeDtypeStruct((UNITS * 8, 128), f32),
        in_specs=scalars(1) + spread(4),
        out_specs=pl.BlockSpec(memory_space=pltpu.VMEM),
        scratch_shapes=[pltpu.VMEM((rows, width), f32)],
        compiler_params=params,
    )(turn_of, gathered, ranks, live, hand_cards)

    chunk = UNITS * 8 // PLANE
    planes = [[k * LINE + z for k in range(PLANE)] for z in range(LINE)]
    lines = [[k * LINE + z for z in range(LINE)] for k in range(PLANE)]

    def copies(blocks, count):
        return pl.pallas_call(
            add_up,
            out_shape=jax.ShapeDtypeStruct((count, chunk, 128), f32),
            in_specs=spread(1),
            out_specs=pl.BlockSpec(memory_space=pltpu.VMEM),
            compiler_params=params,
        )(blocks)

    def swap(blocks, groups):
        return lax.all_to_all(blocks, "turn", 0, 0, axis_index_groups=groups, tiled=True)

    blocks = swap(sums.reshape(PLANE, chunk, 128), planes)
    blocks = swap(copies(blocks, LINE), lines)
    blocks = swap(copies(blocks, PLANE), planes)

    def last(*refs):
        settle(
            turns / boards_all / total_hands, 1.0 / boards_all / total_hands, *refs
        )

    turn_out, flop_out, values = pl.pallas_call(
        last,
        out_shape=(
            jax.ShapeDtypeStruct((actions, turns, width), f32),
            jax.ShapeDtypeStruct((actions, width), f32),
            jax.ShapeDtypeStruct((turns, width), f32),
        ),
        in_specs=spread(3),
        out_specs=tuple(spread(3)),
        compiler_params=params,
    )(blocks.reshape(UNITS * 8, 128), jnp.transpose(turn_regret, (1, 0, 2)), flop_regret)
    return (jnp.transpose(turn_out, (1, 0, 2)), flop_out, values)


def solution(mesh):
    return jax.shard_map(
        shards,
        mesh=mesh,
        in_specs=(
            P("turn", None, "hand"),
            P("turn", "hand"),
            P("turn", "hand"),
            P("turn"),
            P(),
            P(),
            P(),
            P(),
            P(None, None, "hand"),
            P(None, "hand"),
        ),
        out_specs=(P(None, None, "hand"), P(None, "hand"), P(None, "hand")),
        check_vma=False,
    )
```

```python
import jax
import jax.numpy as jnp
from jax import lax
from jax.experimental import pallas as pl
from jax.experimental.pallas import tpu as pltpu
from jax.sharding import PartitionSpec as P

TURNS = 49
SLOTS = 56
UNITS = 128
PLANE = 16
LINE = 8
VMEM = 48 * 1024 * 1024
WHOLE = 60 * 1024 * 1024


def spread(count):
    return [pl.BlockSpec(memory_space=pltpu.VMEM)] * count


def weigh(
    pot_hbm, turn_hbm, flop_hbm, of_hbm, reach_hbm, ranks_hbm, live_hbm, out,
    acc, pot, turn_act, flop_act, turn_of, reach, ranks, live, sems
):
    pairs = (
        (reach_hbm, reach), (pot_hbm, pot), (turn_hbm, turn_act), (flop_hbm, flop_act),
        (of_hbm, turn_of), (ranks_hbm, ranks), (live_hbm, live),
    )
    moves = [pltpu.make_async_copy(x, y, sems.at[k]) for k, (x, y) in enumerate(pairs)]
    for move in moves:
        move.start()
    acc[...] = jnp.zeros_like(acc)
    for move in moves:
        move.wait()
    seqs, boards, width = reach.shape
    half = acc.shape[0] // 2
    for s in range(seqs):
        term = reach[s].astype(jnp.float32) * pot[s]
        acc[turn_act[s]] += term
        acc[half + flop_act[s]] += term
    alive = live[...].astype(jnp.float32)
    for r in range(acc.shape[0]):
        out[pl.ds(r * boards, boards), :] = acc[r] * alive
    top = acc.shape[0] * boards
    out[pl.ds(top, boards), :] = ranks[...].astype(jnp.float32)
    for b in range(boards):
        out[pl.ds(top + boards + b, 1), :] = jnp.full((1, width), turn_of[b], jnp.int32).astype(
            jnp.float32
        )


def showdown(payload, ranks, live, cards, out, acc):
    hands, rows, width = payload.shape
    boards = ranks.shape[0]
    used = rows - 2 * boards
    actions = used // (2 * boards)
    me = lax.axis_index("hand")
    here = cards[:, pl.ds(pl.multiple_of(me * width, width), width)].astype(jnp.float32)
    mine = jnp.concatenate(
        [ranks[...].astype(jnp.float32), here, jnp.zeros((2, width), jnp.float32)], axis=0
    )
    columns = jnp.transpose(mine)
    first, second = columns[:, boards : boards + 1], columns[:, boards + 1 : boards + 2]
    row = lax.broadcasted_iota(jnp.int32, (rows, 1), 0) % boards
    parts = [jnp.zeros((3 * rows, width), jnp.float32) for _ in range(boards)]
    for h in range(hands):
        x = payload[h]
        high = x.astype(jnp.bfloat16)
        rest = x - high.astype(jnp.float32)
        mid = rest.astype(jnp.bfloat16)
        low = (rest - mid.astype(jnp.float32)).astype(jnp.bfloat16)
        pieces = jnp.concatenate([high, mid, low], axis=0)
        there = cards[:, h * width : (h + 1) * width].astype(jnp.float32)
        one, two = there[0:1], there[1:2]
        shared = (first == one) | (first == two) | (second == one) | (second == two)
        apart = jnp.where(shared, 0.0, 1.0)
        for b in range(boards):
            theirs = payload[h, used + b : used + b + 1, :]
            sign = jnp.clip(columns[:, b : b + 1] - theirs, -1.0, 1.0)
            tile = (sign * apart).astype(jnp.bfloat16)
            parts[b] += lax.dot_general(
                pieces, tile, (((1,), (1,)), ((), ())), preferred_element_type=jnp.float32
            )
    total = jnp.zeros((rows, width), jnp.float32)
    for b in range(boards):
        alive = live[b : b + 1, :].astype(jnp.float32)
        part = parts[b][:rows] + (parts[b][rows : 2 * rows] + parts[b][2 * rows :])
        total += jnp.where(row == b, part, 0.0) * alive
    acc[...] = total
    slot = lax.broadcasted_iota(jnp.int32, (SLOTS, 128), 0)
    card = slot.astype(jnp.float32)
    flop_at = used + boards
    hits = [
        (card == payload[0, flop_at + b : flop_at + b + 1, :128]).astype(jnp.float32)
        for b in range(boards)
    ]
    flop = (slot == TURNS).astype(jnp.float32)
    for a in range(actions):
        for half in range(width // 128):
            lanes = pl.ds(half * 128, 128)
            block = jnp.zeros((SLOTS, 128), jnp.float32)
            ends = jnp.zeros((1, 128), jnp.float32)
            for b in range(boards):
                block += hits[b] * acc[a * boards + b : a * boards + b + 1, lanes]
                at = (actions + a) * boards + b
                ends += acc[at : at + 1, lanes]
            block += flop * ends
            out[pl.ds((a * (width // 128) + half) * SLOTS, SLOTS), :] = block
    filled = actions * (width // 128) * SLOTS
    out[pl.ds(filled, UNITS * 8 - filled), :] = jnp.zeros((UNITS * 8 - filled, 128), jnp.float32)


def add_up(blocks, out):
    total = blocks[0]
    for k in range(1, blocks.shape[0]):
        total += blocks[k]
    for k in range(out.shape[0]):
        out[k] = total


def settle(turns_over_boards, over_boards, sums, turn_regret, flop_regret, turn_out, flop_out, values):
    actions, turns, width = turn_regret.shape
    halves = width // 128
    for half in range(halves):
        lanes = pl.ds(half * 128, 128)
        weighted = jnp.zeros((turns, 128), jnp.float32)
        weight = jnp.zeros((turns, 128), jnp.float32)
        top = jnp.zeros((1, 128), jnp.float32)
        bottom = jnp.zeros((1, 128), jnp.float32)
        for a in range(actions):
            base = (a * halves + half) * SLOTS
            regret = turn_regret[a, :, lanes]
            weighted += regret * (sums[pl.ds(base, turns), :] * turns_over_boards)
            weight += regret
            early = flop_regret[a : a + 1, lanes]
            top += early * (sums[pl.ds(base + turns, 1), :] * over_boards)
            bottom += early
        value = weighted / weight
        values[:, lanes] = value
        root = top / bottom
        for a in range(actions):
            base = (a * halves + half) * SLOTS
            q = sums[pl.ds(base, turns), :] * turns_over_boards
            turn_out[a, :, lanes] = jnp.maximum(turn_regret[a, :, lanes] + q - value, 0.0)
            q = sums[pl.ds(base + turns, 1), :] * over_boards
            flop_out[a : a + 1, lanes] = jnp.maximum(flop_regret[a : a + 1, lanes] + q - root, 0.0)


def shards(
    reach, ranks, live, turn_of, hand_cards, pot, turn_act, flop_act, turn_regret, flop_regret
):
    boards, seqs, width = reach.shape
    total_hands = hand_cards.shape[1]
    turns, actions, _ = turn_regret.shape
    rows = 2 * actions * boards
    boards_all = boards * lax.axis_size("turn")
    params = pltpu.CompilerParams(vmem_limit_bytes=VMEM)
    f32 = jnp.float32

    payload = pl.pallas_call(
        weigh,
        out_shape=jax.ShapeDtypeStruct((rows + 2 * boards, width), f32),
        in_specs=[pl.BlockSpec(memory_space=pltpu.HBM)] * 7,
        out_specs=pl.BlockSpec(memory_space=pltpu.VMEM),
        scratch_shapes=[
            pltpu.VMEM((2 * actions, boards, width), f32),
            pltpu.SMEM(pot.shape, f32),
            pltpu.SMEM(turn_act.shape, jnp.int32),
            pltpu.SMEM(flop_act.shape, jnp.int32),
            pltpu.SMEM(turn_of.shape, jnp.int32),
            pltpu.VMEM((seqs, boards, width), reach.dtype),
            pltpu.VMEM(ranks.shape, jnp.int32),
            pltpu.VMEM(live.shape, jnp.int32),
            pltpu.SemaphoreType.DMA((7,)),
        ],
        compiler_params=pltpu.CompilerParams(vmem_limit_bytes=WHOLE),
    )(pot, turn_act, flop_act, turn_of, jnp.transpose(reach, (1, 0, 2)), ranks, live)

    gathered = lax.all_gather(payload, "hand", axis=0, tiled=False)

    sums = pl.pallas_call(
        showdown,
        out_shape=jax.ShapeDtypeStruct((UNITS * 8, 128), f32),
        in_specs=spread(4),
        out_specs=pl.BlockSpec(memory_space=pltpu.VMEM),
        scratch_shapes=[pltpu.VMEM((rows + 2 * boards, width), f32)],
        compiler_params=params,
    )(gathered, ranks, live, hand_cards)

    chunk = UNITS * 8 // PLANE
    planes = [[k * LINE + z for k in range(PLANE)] for z in range(LINE)]
    lines = [[k * LINE + z for z in range(LINE)] for k in range(PLANE)]

    def copies(blocks, count):
        return pl.pallas_call(
            add_up,
            out_shape=jax.ShapeDtypeStruct((count, chunk, 128), f32),
            in_specs=spread(1),
            out_specs=pl.BlockSpec(memory_space=pltpu.VMEM),
            compiler_params=params,
        )(blocks)

    def swap(blocks, groups):
        return lax.all_to_all(blocks, "turn", 0, 0, axis_index_groups=groups, tiled=True)

    blocks = swap(sums.reshape(PLANE, chunk, 128), planes)
    blocks = swap(copies(blocks, LINE), lines)
    blocks = swap(copies(blocks, PLANE), planes)

    def last(*refs):
        settle(
            turns / boards_all / total_hands, 1.0 / boards_all / total_hands, *refs
        )

    turn_out, flop_out, values = pl.pallas_call(
        last,
        out_shape=(
            jax.ShapeDtypeStruct((actions, turns, width), f32),
            jax.ShapeDtypeStruct((actions, width), f32),
            jax.ShapeDtypeStruct((turns, width), f32),
        ),
        in_specs=spread(3),
        out_specs=tuple(spread(3)),
        compiler_params=params,
    )(blocks.reshape(UNITS * 8, 128), jnp.transpose(turn_regret, (1, 0, 2)), flop_regret)
    return (jnp.transpose(turn_out, (1, 0, 2)), flop_out, values)


def solution(mesh):
    return jax.shard_map(
        shards,
        mesh=mesh,
        in_specs=(
            P("turn", None, "hand"),
            P("turn", "hand"),
            P("turn", "hand"),
            P("turn"),
            P(),
            P(),
            P(),
            P(),
            P(None, None, "hand"),
            P(None, "hand"),
        ),
        out_specs=(P(None, None, "hand"), P(None, "hand"), P(None, "hand")),
        check_vma=False,
    )
```

```python
import jax
import jax.numpy as jnp
from jax import lax
from jax.experimental import pallas as pl
from jax.experimental.pallas import tpu as pltpu
from jax.sharding import PartitionSpec as P

TURNS = 49
SLOTS = 56
UNITS = 128
PLANE = 16
LINE = 8
CHUNK = UNITS * 8 // PLANE
STEPS = 32760.0
VMEM = 48 * 1024 * 1024
WHOLE = 60 * 1024 * 1024


def spread(count):
    return [pl.BlockSpec(memory_space=pltpu.VMEM)] * count


def pack(x, out, k):
    rows = x.shape[0]
    lane = lax.broadcasted_iota(jnp.int32, (16, 128), 1) // 32
    top = jnp.maximum(jnp.max(jnp.abs(x), axis=1, keepdims=True), 1e-30)
    log = jnp.ceil(jnp.log2(top) * 256.0)
    codes = jnp.round(x * (STEPS / jnp.exp2(log * (1.0 / 256.0))))
    out[k, :rows, :] = codes.astype(jnp.int32).astype(jnp.int16)
    logs = jnp.zeros((16, 128), jnp.float32)
    for g in range(rows // 16):
        logs = jnp.where(lane == g, log[16 * g : 16 * g + 16], logs)
    out[k, rows:, :] = logs.astype(jnp.int32).astype(jnp.int16)


def unpack(block):
    codes = block[:64].astype(jnp.int32).astype(jnp.float32)
    logs = block[64:].astype(jnp.int32).astype(jnp.float32)
    scale = jnp.exp2(logs * (1.0 / 256.0)) * (1.0 / STEPS)
    return jnp.concatenate(
        [codes[16 * g : 16 * g + 16] * scale[:, 32 * g : 32 * g + 1] for g in range(4)], axis=0
    )


def weigh(
    pot_hbm, turn_hbm, flop_hbm, of_hbm, reach_hbm, ranks_hbm, live_hbm, out,
    acc, pot, turn_act, flop_act, turn_of, reach, ranks, live, sems
):
    pairs = (
        (reach_hbm, reach), (pot_hbm, pot), (turn_hbm, turn_act), (flop_hbm, flop_act),
        (of_hbm, turn_of), (ranks_hbm, ranks), (live_hbm, live),
    )
    moves = [pltpu.make_async_copy(x, y, sems.at[k]) for k, (x, y) in enumerate(pairs)]
    for move in moves:
        move.start()
    acc[...] = jnp.zeros_like(acc)
    for move in moves:
        move.wait()
    seqs, boards, width = reach.shape
    half = acc.shape[0] // 2
    for s in range(seqs):
        term = reach[s].astype(jnp.float32) * pot[s]
        acc[turn_act[s]] += term
        acc[half + flop_act[s]] += term
    alive = live[...].astype(jnp.float32)
    for r in range(acc.shape[0]):
        out[pl.ds(r * boards, boards), :] = acc[r] * alive
    top = acc.shape[0] * boards
    out[pl.ds(top, boards), :] = ranks[...].astype(jnp.float32)
    for b in range(boards):
        out[pl.ds(top + boards + b, 1), :] = jnp.full((1, width), turn_of[b], jnp.int32).astype(
            jnp.float32
        )


def showdown(payload, ranks, live, cards, out, acc, dense):
    hands, rows, width = payload.shape
    boards = ranks.shape[0]
    used = rows - 2 * boards
    actions = used // (2 * boards)
    me = lax.axis_index("hand")
    here = cards[:, pl.ds(pl.multiple_of(me * width, width), width)].astype(jnp.float32)
    mine = jnp.concatenate(
        [ranks[...].astype(jnp.float32), here, jnp.zeros((2, width), jnp.float32)], axis=0
    )
    columns = jnp.transpose(mine)
    first, second = columns[:, boards : boards + 1], columns[:, boards + 1 : boards + 2]
    row = lax.broadcasted_iota(jnp.int32, (rows, 1), 0) % boards
    parts = [jnp.zeros((3 * rows, width), jnp.float32) for _ in range(boards)]
    for h in range(hands):
        x = payload[h]
        high = x.astype(jnp.bfloat16)
        rest = x - high.astype(jnp.float32)
        mid = rest.astype(jnp.bfloat16)
        low = (rest - mid.astype(jnp.float32)).astype(jnp.bfloat16)
        pieces = jnp.concatenate([high, mid, low], axis=0)
        there = cards[:, h * width : (h + 1) * width].astype(jnp.float32)
        one, two = there[0:1], there[1:2]
        shared = (first == one) | (first == two) | (second == one) | (second == two)
        apart = jnp.where(shared, 0.0, 1.0)
        for b in range(boards):
            theirs = payload[h, used + b : used + b + 1, :]
            sign = jnp.clip(columns[:, b : b + 1] - theirs, -1.0, 1.0)
            tile = (sign * apart).astype(jnp.bfloat16)
            parts[b] += lax.dot_general(
                pieces, tile, (((1,), (1,)), ((), ())), preferred_element_type=jnp.float32
            )
    total = jnp.zeros((rows, width), jnp.float32)
    for b in range(boards):
        alive = live[b : b + 1, :].astype(jnp.float32)
        part = parts[b][:rows] + (parts[b][rows : 2 * rows] + parts[b][2 * rows :])
        total += jnp.where(row == b, part, 0.0) * alive
    acc[...] = total
    slot = lax.broadcasted_iota(jnp.int32, (SLOTS, 128), 0)
    card = slot.astype(jnp.float32)
    flop_at = used + boards
    hits = [
        (card == payload[0, flop_at + b : flop_at + b + 1, :128]).astype(jnp.float32)
        for b in range(boards)
    ]
    flop = (slot == TURNS).astype(jnp.float32)
    for a in range(actions):
        for half in range(width // 128):
            lanes = pl.ds(half * 128, 128)
            block = jnp.zeros((SLOTS, 128), jnp.float32)
            ends = jnp.zeros((1, 128), jnp.float32)
            for b in range(boards):
                block += hits[b] * acc[a * boards + b : a * boards + b + 1, lanes]
                at = (actions + a) * boards + b
                ends += acc[at : at + 1, lanes]
            block += flop * ends
            dense[pl.ds((a * (width // 128) + half) * SLOTS, SLOTS), :] = block
    filled = actions * (width // 128) * SLOTS
    dense[pl.ds(filled, UNITS * 8 - filled), :] = jnp.zeros((UNITS * 8 - filled, 128), jnp.float32)
    for k in range(PLANE):
        pack(dense[pl.ds(k * CHUNK, CHUNK), :], out, k)


def add_up(blocks, out):
    total = unpack(blocks[0])
    for k in range(1, blocks.shape[0]):
        total += unpack(blocks[k])
    pack(total, out, 0)
    for k in range(1, out.shape[0]):
        out[k] = out[0]


def settle(turns_over_boards, over_boards, blocks, turn_regret, flop_regret, turn_out, flop_out, values, sums):
    for k in range(PLANE):
        sums[pl.ds(k * CHUNK, CHUNK), :] = unpack(blocks[k])
    actions, turns, width = turn_regret.shape
    halves = width // 128
    for half in range(halves):
        lanes = pl.ds(half * 128, 128)
        weighted = jnp.zeros((turns, 128), jnp.float32)
        weight = jnp.zeros((turns, 128), jnp.float32)
        top = jnp.zeros((1, 128), jnp.float32)
        bottom = jnp.zeros((1, 128), jnp.float32)
        for a in range(actions):
            base = (a * halves + half) * SLOTS
            regret = turn_regret[a, :, lanes]
            weighted += regret * (sums[pl.ds(base, turns), :] * turns_over_boards)
            weight += regret
            early = flop_regret[a : a + 1, lanes]
            top += early * (sums[pl.ds(base + turns, 1), :] * over_boards)
            bottom += early
        value = weighted / weight
        values[:, lanes] = value
        root = top / bottom
        for a in range(actions):
            base = (a * halves + half) * SLOTS
            q = sums[pl.ds(base, turns), :] * turns_over_boards
            turn_out[a, :, lanes] = jnp.maximum(turn_regret[a, :, lanes] + q - value, 0.0)
            q = sums[pl.ds(base + turns, 1), :] * over_boards
            flop_out[a : a + 1, lanes] = jnp.maximum(flop_regret[a : a + 1, lanes] + q - root, 0.0)


def shards(
    reach, ranks, live, turn_of, hand_cards, pot, turn_act, flop_act, turn_regret, flop_regret
):
    boards, seqs, width = reach.shape
    total_hands = hand_cards.shape[1]
    turns, actions, _ = turn_regret.shape
    rows = 2 * actions * boards
    boards_all = boards * lax.axis_size("turn")
    params = pltpu.CompilerParams(vmem_limit_bytes=VMEM)
    f32 = jnp.float32

    payload = pl.pallas_call(
        weigh,
        out_shape=jax.ShapeDtypeStruct((rows + 2 * boards, width), f32),
        in_specs=[pl.BlockSpec(memory_space=pltpu.HBM)] * 7,
        out_specs=pl.BlockSpec(memory_space=pltpu.VMEM),
        scratch_shapes=[
            pltpu.VMEM((2 * actions, boards, width), f32),
            pltpu.SMEM(pot.shape, f32),
            pltpu.SMEM(turn_act.shape, jnp.int32),
            pltpu.SMEM(flop_act.shape, jnp.int32),
            pltpu.SMEM(turn_of.shape, jnp.int32),
            pltpu.VMEM((seqs, boards, width), reach.dtype),
            pltpu.VMEM(ranks.shape, jnp.int32),
            pltpu.VMEM(live.shape, jnp.int32),
            pltpu.SemaphoreType.DMA((7,)),
        ],
        compiler_params=pltpu.CompilerParams(vmem_limit_bytes=WHOLE),
    )(pot, turn_act, flop_act, turn_of, jnp.transpose(reach, (1, 0, 2)), ranks, live)

    gathered = lax.all_gather(payload, "hand", axis=0, tiled=False)

    sums = pl.pallas_call(
        showdown,
        out_shape=jax.ShapeDtypeStruct((PLANE, CHUNK + 16, 128), jnp.int16),
        in_specs=spread(4),
        out_specs=pl.BlockSpec(memory_space=pltpu.VMEM),
        scratch_shapes=[
            pltpu.VMEM((rows + 2 * boards, width), f32),
            pltpu.VMEM((UNITS * 8, 128), f32),
        ],
        compiler_params=params,
    )(gathered, ranks, live, hand_cards)

    planes = [[k * LINE + z for k in range(PLANE)] for z in range(LINE)]
    lines = [[k * LINE + z for z in range(LINE)] for k in range(PLANE)]

    def copies(blocks, count):
        return pl.pallas_call(
            add_up,
            out_shape=jax.ShapeDtypeStruct((count, CHUNK + 16, 128), jnp.int16),
            in_specs=spread(1),
            out_specs=pl.BlockSpec(memory_space=pltpu.VMEM),
            compiler_params=params,
        )(blocks)

    def swap(blocks, groups):
        return lax.all_to_all(blocks, "turn", 0, 0, axis_index_groups=groups, tiled=True)

    blocks = swap(sums, planes)
    blocks = swap(copies(blocks, LINE), lines)
    blocks = swap(copies(blocks, PLANE), planes)

    def last(*refs):
        settle(
            turns / boards_all / total_hands, 1.0 / boards_all / total_hands, *refs
        )

    turn_out, flop_out, values = pl.pallas_call(
        last,
        out_shape=(
            jax.ShapeDtypeStruct((actions, turns, width), f32),
            jax.ShapeDtypeStruct((actions, width), f32),
            jax.ShapeDtypeStruct((turns, width), f32),
        ),
        in_specs=spread(3),
        out_specs=tuple(spread(3)),
        scratch_shapes=[pltpu.VMEM((UNITS * 8, 128), f32)],
        compiler_params=params,
    )(blocks, jnp.transpose(turn_regret, (1, 0, 2)), flop_regret)
    return (jnp.transpose(turn_out, (1, 0, 2)), flop_out, values)


def solution(mesh):
    return jax.shard_map(
        shards,
        mesh=mesh,
        in_specs=(
            P("turn", None, "hand"),
            P("turn", "hand"),
            P("turn", "hand"),
            P("turn"),
            P(),
            P(),
            P(),
            P(),
            P(None, None, "hand"),
            P(None, "hand"),
        ),
        out_specs=(P(None, None, "hand"), P(None, "hand"), P(None, "hand")),
        check_vma=False,
    )
```

```python
import jax
import jax.numpy as jnp
from jax import lax
from jax.experimental import pallas as pl
from jax.experimental.pallas import tpu as pltpu
from jax.sharding import PartitionSpec as P

TURNS = 49
SLOTS = 56
UNITS = 128
PLANE = 16
LINE = 8
CHUNK = UNITS * 8 // PLANE
STEPS = 32760.0
SCALES = 58
VMEM = 48 * 1024 * 1024
WHOLE = 60 * 1024 * 1024


def spread(count):
    return [pl.BlockSpec(memory_space=pltpu.VMEM)] * count


def place(column, tile):
    columns, tiles = UNITS // (SLOTS // 8), SLOTS // 8
    if tile == tiles - 1 and column < PLANE:
        return column * CHUNK + CHUNK - 8
    spot = column * (tiles - 1) + tile if tile < tiles - 1 else columns * (tiles - 1) + column - PLANE
    return spot // 7 * CHUNK + spot % 7 * 8


def pack(x):
    row = lax.broadcasted_iota(jnp.int32, x.shape, 0)
    lane = lax.broadcasted_iota(jnp.int32, x.shape, 1)
    top = jnp.maximum(jnp.max(jnp.abs(x), axis=1, keepdims=True), 1e-30)
    log = jnp.ceil(jnp.log2(top) * 256.0)
    codes = jnp.round(x * (STEPS / jnp.exp2(log * (1.0 / 256.0))))
    logs = jnp.sum(jnp.where(row == lane, log, 0.0), axis=0, keepdims=True)
    return jnp.where(row == SCALES, logs, codes).astype(jnp.int32).astype(jnp.int16)


def unpack(blocks):
    count = blocks.shape[0]
    ends = [blocks[k, 48:64, :].astype(jnp.int32).astype(jnp.float32) for k in range(count)]
    logs = jnp.concatenate([end[SCALES - 48 : SCALES - 47] for end in ends], axis=0)
    scales = jnp.transpose(jnp.exp2(logs * (1.0 / 256.0)) * (1.0 / STEPS))
    for k in range(count):
        codes = blocks[k].astype(jnp.int32).astype(jnp.float32)
        yield codes * scales[:64, k : k + 1]


def weigh(
    pot_hbm, turn_hbm, flop_hbm, of_hbm, reach_hbm, ranks_hbm, live_hbm, out,
    acc, pot, turn_act, flop_act, turn_of, reach, ranks, live, sems
):
    pairs = (
        (reach_hbm, reach), (pot_hbm, pot), (turn_hbm, turn_act), (flop_hbm, flop_act),
        (of_hbm, turn_of), (ranks_hbm, ranks), (live_hbm, live),
    )
    moves = [pltpu.make_async_copy(x, y, sems.at[k]) for k, (x, y) in enumerate(pairs)]
    for move in moves:
        move.start()
    acc[...] = jnp.zeros_like(acc)
    for move in moves:
        move.wait()
    seqs, boards, width = reach.shape
    half = acc.shape[0] // 2
    for s in range(seqs):
        term = reach[s].astype(jnp.float32) * pot[s]
        acc[turn_act[s]] += term
        acc[half + flop_act[s]] += term
    alive = live[...].astype(jnp.float32)
    for r in range(acc.shape[0]):
        out[pl.ds(r * boards, boards), :] = acc[r] * alive
    top = acc.shape[0] * boards
    out[pl.ds(top, boards), :] = ranks[...].astype(jnp.float32)
    for b in range(boards):
        out[pl.ds(top + boards + b, 1), :] = jnp.full((1, width), turn_of[b], jnp.int32).astype(
            jnp.float32
        )


def showdown(payload, ranks, live, cards, out, acc, dense):
    hands, rows, width = payload.shape
    boards = ranks.shape[0]
    used = rows - 2 * boards
    actions = used // (2 * boards)
    me = lax.axis_index("hand")
    here = cards[:, pl.ds(pl.multiple_of(me * width, width), width)].astype(jnp.float32)
    mine = jnp.concatenate(
        [ranks[...].astype(jnp.float32), here, jnp.zeros((2, width), jnp.float32)], axis=0
    )
    columns = jnp.transpose(mine)
    first, second = columns[:, boards : boards + 1], columns[:, boards + 1 : boards + 2]
    row = lax.broadcasted_iota(jnp.int32, (rows, 1), 0) % boards
    parts = [jnp.zeros((3 * rows, width), jnp.float32) for _ in range(boards)]
    for h in range(hands):
        x = payload[h]
        high = x.astype(jnp.bfloat16)
        rest = x - high.astype(jnp.float32)
        mid = rest.astype(jnp.bfloat16)
        low = (rest - mid.astype(jnp.float32)).astype(jnp.bfloat16)
        pieces = jnp.concatenate([high, mid, low], axis=0)
        there = cards[:, h * width : (h + 1) * width].astype(jnp.float32)
        one, two = there[0:1], there[1:2]
        shared = (first == one) | (first == two) | (second == one) | (second == two)
        apart = jnp.where(shared, 0.0, 1.0)
        for b in range(boards):
            theirs = payload[h, used + b : used + b + 1, :]
            sign = jnp.clip(columns[:, b : b + 1] - theirs, -1.0, 1.0)
            tile = (sign * apart).astype(jnp.bfloat16)
            parts[b] += lax.dot_general(
                pieces, tile, (((1,), (1,)), ((), ())), preferred_element_type=jnp.float32
            )
    total = jnp.zeros((rows, width), jnp.float32)
    for b in range(boards):
        alive = live[b : b + 1, :].astype(jnp.float32)
        part = parts[b][:rows] + (parts[b][rows : 2 * rows] + parts[b][2 * rows :])
        total += jnp.where(row == b, part, 0.0) * alive
    acc[...] = total
    slot = lax.broadcasted_iota(jnp.int32, (SLOTS, 128), 0)
    card = slot.astype(jnp.float32)
    flop_at = used + boards
    hits = [
        (card == payload[0, flop_at + b : flop_at + b + 1, :128]).astype(jnp.float32)
        for b in range(boards)
    ]
    flop = (slot == TURNS).astype(jnp.float32)
    for a in range(actions):
        for half in range(width // 128):
            lanes = pl.ds(half * 128, 128)
            block = jnp.zeros((SLOTS, 128), jnp.float32)
            ends = jnp.zeros((1, 128), jnp.float32)
            for b in range(boards):
                block += hits[b] * acc[a * boards + b : a * boards + b + 1, lanes]
                at = (actions + a) * boards + b
                ends += acc[at : at + 1, lanes]
            block += flop * ends
            column = a * (width // 128) + half
            for tile in range(SLOTS // 8):
                dense[pl.ds(place(column, tile), 8), :] = block[tile * 8 : tile * 8 + 8]
    spots = {place(c, t) for c in range(actions * (width // 128)) for t in range(SLOTS // 8)}
    for spot in sorted(set(range(0, UNITS * 8, 8)) - spots):
        dense[pl.ds(spot, 8), :] = jnp.zeros((8, 128), jnp.float32)
    for k in range(PLANE):
        out[k] = pack(dense[pl.ds(k * CHUNK, CHUNK), :])


def add_up(blocks, out):
    total = jnp.zeros((CHUNK, 128), jnp.float32)
    for block in unpack(blocks):
        total += block
    row = lax.broadcasted_iota(jnp.int32, total.shape, 0)
    codes = pack(jnp.where(row == SCALES, 0.0, total))
    for k in range(out.shape[0]):
        out[k] = codes


def settle(turns_over_boards, over_boards, blocks, turn_regret, flop_regret, turn_out, flop_out, values, sums):
    actions, turns, width = turn_regret.shape
    halves = width // 128
    for k, block in enumerate(unpack(blocks)):
        sums[pl.ds(k * CHUNK, CHUNK), :] = block

    def column(at):
        tiles = [sums[pl.ds(place(at, tile), 8), :] for tile in range(SLOTS // 8)]
        whole = jnp.concatenate(tiles, axis=0)
        return whole[:turns] * turns_over_boards, whole[turns : turns + 1] * over_boards

    for half in range(halves):
        lanes = pl.ds(half * 128, 128)
        weighted = jnp.zeros((turns, 128), jnp.float32)
        weight = jnp.zeros((turns, 128), jnp.float32)
        top = jnp.zeros((1, 128), jnp.float32)
        bottom = jnp.zeros((1, 128), jnp.float32)
        for a in range(actions):
            q, flop_q = column(a * halves + half)
            regret = turn_regret[a, :, lanes]
            weighted += regret * q
            weight += regret
            early = flop_regret[a : a + 1, lanes]
            top += early * flop_q
            bottom += early
        value = weighted / weight
        values[:, lanes] = value
        root = top / bottom
        for a in range(actions):
            q, flop_q = column(a * halves + half)
            turn_out[a, :, lanes] = jnp.maximum(turn_regret[a, :, lanes] + q - value, 0.0)
            early = flop_regret[a : a + 1, lanes]
            flop_out[a : a + 1, lanes] = jnp.maximum(early + flop_q - root, 0.0)


def shards(
    reach, ranks, live, turn_of, hand_cards, pot, turn_act, flop_act, turn_regret, flop_regret
):
    boards, seqs, width = reach.shape
    total_hands = hand_cards.shape[1]
    turns, actions, _ = turn_regret.shape
    rows = 2 * actions * boards
    boards_all = boards * lax.axis_size("turn")
    params = pltpu.CompilerParams(vmem_limit_bytes=VMEM)
    f32 = jnp.float32

    payload = pl.pallas_call(
        weigh,
        out_shape=jax.ShapeDtypeStruct((rows + 2 * boards, width), f32),
        in_specs=[pl.BlockSpec(memory_space=pltpu.HBM)] * 7,
        out_specs=pl.BlockSpec(memory_space=pltpu.VMEM),
        scratch_shapes=[
            pltpu.VMEM((2 * actions, boards, width), f32),
            pltpu.SMEM(pot.shape, f32),
            pltpu.SMEM(turn_act.shape, jnp.int32),
            pltpu.SMEM(flop_act.shape, jnp.int32),
            pltpu.SMEM(turn_of.shape, jnp.int32),
            pltpu.VMEM((seqs, boards, width), reach.dtype),
            pltpu.VMEM(ranks.shape, jnp.int32),
            pltpu.VMEM(live.shape, jnp.int32),
            pltpu.SemaphoreType.DMA((7,)),
        ],
        compiler_params=pltpu.CompilerParams(vmem_limit_bytes=WHOLE),
    )(pot, turn_act, flop_act, turn_of, jnp.transpose(reach, (1, 0, 2)), ranks, live)

    gathered = lax.all_gather(payload, "hand", axis=0, tiled=False)

    sums = pl.pallas_call(
        showdown,
        out_shape=jax.ShapeDtypeStruct((PLANE, CHUNK, 128), jnp.int16),
        in_specs=spread(4),
        out_specs=pl.BlockSpec(memory_space=pltpu.VMEM),
        scratch_shapes=[
            pltpu.VMEM((rows + 2 * boards, width), f32),
            pltpu.VMEM((UNITS * 8, 128), f32),
        ],
        compiler_params=params,
    )(gathered, ranks, live, hand_cards)

    planes = [[k * LINE + z for k in range(PLANE)] for z in range(LINE)]
    lines = [[k * LINE + z for z in range(LINE)] for k in range(PLANE)]

    def copies(blocks, count):
        return pl.pallas_call(
            add_up,
            out_shape=jax.ShapeDtypeStruct((count, CHUNK, 128), jnp.int16),
            in_specs=spread(1),
            out_specs=pl.BlockSpec(memory_space=pltpu.VMEM),
            compiler_params=params,
        )(blocks)

    def swap(blocks, groups):
        return lax.all_to_all(blocks, "turn", 0, 0, axis_index_groups=groups, tiled=True)

    blocks = swap(sums, planes)
    blocks = swap(copies(blocks, LINE), lines)
    blocks = swap(copies(blocks, PLANE), planes)

    def last(*refs):
        settle(
            turns / boards_all / total_hands, 1.0 / boards_all / total_hands, *refs
        )

    turn_out, flop_out, values = pl.pallas_call(
        last,
        out_shape=(
            jax.ShapeDtypeStruct((actions, turns, width), f32),
            jax.ShapeDtypeStruct((actions, width), f32),
            jax.ShapeDtypeStruct((turns, width), f32),
        ),
        in_specs=spread(3),
        out_specs=tuple(spread(3)),
        scratch_shapes=[pltpu.VMEM((UNITS * 8, 128), f32)],
        compiler_params=params,
    )(blocks, jnp.transpose(turn_regret, (1, 0, 2)), flop_regret)
    return (jnp.transpose(turn_out, (1, 0, 2)), flop_out, values)


def solution(mesh):
    return jax.shard_map(
        shards,
        mesh=mesh,
        in_specs=(
            P("turn", None, "hand"),
            P("turn", "hand"),
            P("turn", "hand"),
            P("turn"),
            P(),
            P(),
            P(),
            P(),
            P(None, None, "hand"),
            P(None, "hand"),
        ),
        out_specs=(P(None, None, "hand"), P(None, "hand"), P(None, "hand")),
        check_vma=False,
    )
```

```python
import jax
import jax.numpy as jnp
from jax import lax
from jax.experimental import pallas as pl
from jax.experimental.pallas import tpu as pltpu
from jax.sharding import PartitionSpec as P

TURNS = 49
SLOTS = 56
UNITS = 128
PLANE = 16
LINE = 8
CHUNK = UNITS * 8 // PLANE
STEPS = 32760.0
SCALES = 58
VMEM = 48 * 1024 * 1024
BANKS = 4


def spread(count):
    return [pl.BlockSpec(memory_space=pltpu.VMEM)] * count


def place(column, tile):
    columns, tiles = UNITS // (SLOTS // 8), SLOTS // 8
    if tile == tiles - 1 and column < PLANE:
        return column * CHUNK + CHUNK - 8
    spot = column * (tiles - 1) + tile if tile < tiles - 1 else columns * (tiles - 1) + column - PLANE
    return spot // 7 * CHUNK + spot % 7 * 8


def pack(x):
    row = lax.broadcasted_iota(jnp.int32, x.shape, 0)
    lane = lax.broadcasted_iota(jnp.int32, x.shape, 1)
    top = jnp.maximum(jnp.max(jnp.abs(x), axis=1, keepdims=True), 1e-30)
    log = jnp.ceil(jnp.log2(top) * 256.0)
    codes = jnp.round(x * (STEPS / jnp.exp2(log * (1.0 / 256.0))))
    logs = jnp.sum(jnp.where(row == lane, log, 0.0), axis=0, keepdims=True)
    return jnp.where(row == SCALES, logs, codes).astype(jnp.int32).astype(jnp.int16)


def unpack(blocks):
    count = blocks.shape[0]
    ends = [blocks[k, 48:64, :].astype(jnp.int32).astype(jnp.float32) for k in range(count)]
    logs = jnp.concatenate([end[SCALES - 48 : SCALES - 47] for end in ends], axis=0)
    scales = jnp.transpose(jnp.exp2(logs * (1.0 / 256.0)) * (1.0 / STEPS))
    for k in range(count):
        codes = blocks[k].astype(jnp.int32).astype(jnp.float32)
        yield codes * scales[:64, k : k + 1]


def weigh(
    pot_hbm, turn_hbm, flop_hbm, of_hbm, reach_hbm, ranks_hbm, live_hbm, out,
    pot, turn_act, flop_act, turn_of, reach, ranks, live, sems, *banks
):
    pairs = (
        (reach_hbm, reach), (pot_hbm, pot), (turn_hbm, turn_act), (flop_hbm, flop_act),
        (of_hbm, turn_of), (ranks_hbm, ranks), (live_hbm, live),
    )
    moves = [pltpu.make_async_copy(x, y, sems.at[k]) for k, (x, y) in enumerate(pairs)]
    for move in moves:
        move.start()
    turn_sums, flop_sums = banks[:BANKS], banks[BANKS:]
    for bank in banks:
        bank[...] = jnp.zeros_like(bank)
    for move in moves:
        move.wait()
    seqs, boards, width = reach.shape
    halves = [slice(half * 128, half * 128 + 128) for half in range(width // 128)]
    for s in range(seqs):
        term = reach[s].astype(jnp.float32) * pot[s]
        turn_sums[s % BANKS][turn_act[s]] += term
        flop_sums[s % BANKS][flop_act[s]] += term
    alive = live[...].astype(jnp.float32)
    top = 0
    for sums in (turn_sums, flop_sums):
        for r in range(sums[0].shape[0]):
            total = sums[0][r]
            for other in sums[1:]:
                total += other[r]
            total *= alive
            for half, lanes in enumerate(halves):
                out[half, pl.ds(top, boards), :] = total[:, lanes]
            top += boards
    for half, lanes in enumerate(halves):
        out[half, pl.ds(top, boards), :] = ranks[:, lanes].astype(jnp.float32)
        for b in range(boards):
            card = jnp.full((1, 128), turn_of[b], jnp.int32).astype(jnp.float32)
            out[half, pl.ds(top + boards + b, 1), :] = card


def showdown(payload, ranks, live, cards, out, dense):
    hands, halves, rows, _ = payload.shape
    width = halves * 128
    boards = ranks.shape[0]
    each = rows // boards
    actions = (each - 2) // 2
    me = lax.axis_index("hand")
    here = cards[:, pl.ds(pl.multiple_of(me * width, width), width)].astype(jnp.float32)
    mine = jnp.concatenate(
        [ranks[...].astype(jnp.float32), here, jnp.zeros((2, width), jnp.float32)], axis=0
    )
    columns = jnp.transpose(mine)
    first, second = columns[:, boards : boards + 1], columns[:, boards + 1 : boards + 2]
    aparts = []
    for h in range(hands):
        there = cards[:, h * width : (h + 1) * width].astype(jnp.float32)
        one, two = there[0:1], there[1:2]
        shared = (first == one) | (first == two) | (second == one) | (second == two)
        aparts.append(jnp.where(shared, 0.0, 1.0))
    apart = jnp.concatenate(aparts, axis=1)
    tall = -(-each // 8) * 8
    sums = []
    slot = lax.broadcasted_iota(jnp.int32, (SLOTS, 128), 0)
    card = slot.astype(jnp.float32)
    hits = []
    for b in range(boards):
        x = jnp.concatenate(
            [payload[h, half, pl.ds(b, each, stride=boards), :] for h in range(hands) for half in range(halves)],
            axis=1,
        )
        theirs = x[each - 2 : each - 1]
        hits.append((card == x[each - 1 : each, :128]).astype(jnp.float32))
        x = jnp.concatenate([x, jnp.zeros((tall - each, hands * width), jnp.float32)], axis=0)
        high = x.astype(jnp.bfloat16).astype(jnp.float32)
        mid = (x - high).astype(jnp.bfloat16).astype(jnp.float32)
        pieces = jnp.concatenate([high, mid, x - high - mid], axis=0).astype(jnp.bfloat16)
        sign = jnp.clip(columns[:, b : b + 1] - theirs, -1.0, 1.0)
        tile = (sign * apart).astype(jnp.bfloat16)
        part = lax.dot_general(
            pieces, tile, (((1,), (1,)), ((), ())), preferred_element_type=jnp.float32
        )
        part = part[:tall] + (part[tall : 2 * tall] + part[2 * tall :])
        sums.append(part * live[b : b + 1, :].astype(jnp.float32))
    flops = sums[0]
    for b in range(1, boards):
        flops += sums[b]
    flop = (slot == TURNS).astype(jnp.float32)
    for a in range(actions):
        for half in range(width // 128):
            lanes = slice(half * 128, half * 128 + 128)
            block = flop * flops[actions + a : actions + a + 1, lanes]
            for b in range(boards):
                block += hits[b] * sums[b][a : a + 1, lanes]
            column = a * (width // 128) + half
            for tile in range(SLOTS // 8):
                dense[pl.ds(place(column, tile), 8), :] = block[tile * 8 : tile * 8 + 8]
    spots = {place(c, t) for c in range(actions * (width // 128)) for t in range(SLOTS // 8)}
    for spot in sorted(set(range(0, UNITS * 8, 8)) - spots):
        dense[pl.ds(spot, 8), :] = jnp.zeros((8, 128), jnp.float32)
    for k in range(PLANE):
        out[k] = pack(dense[pl.ds(k * CHUNK, CHUNK), :])


def add_up(blocks, out):
    total = jnp.zeros((CHUNK, 128), jnp.float32)
    for block in unpack(blocks):
        total += block
    row = lax.broadcasted_iota(jnp.int32, total.shape, 0)
    codes = pack(jnp.where(row == SCALES, 0.0, total))
    for k in range(out.shape[0]):
        out[k] = codes


def settle(turns_over_boards, over_boards, blocks, turn_regret, flop_regret, turn_out, flop_out, values, sums):
    actions, turns, width = turn_regret.shape
    halves = width // 128
    for k, block in enumerate(unpack(blocks)):
        sums[pl.ds(k * CHUNK, CHUNK), :] = block

    def column(at):
        tiles = [sums[pl.ds(place(at, tile), 8), :] for tile in range(SLOTS // 8)]
        whole = jnp.concatenate(tiles, axis=0)
        return whole[:turns] * turns_over_boards, whole[turns : turns + 1] * over_boards

    for half in range(halves):
        lanes = pl.ds(half * 128, 128)
        weighted = jnp.zeros((turns, 128), jnp.float32)
        weight = jnp.zeros((turns, 128), jnp.float32)
        top = jnp.zeros((1, 128), jnp.float32)
        bottom = jnp.zeros((1, 128), jnp.float32)
        for a in range(actions):
            q, flop_q = column(a * halves + half)
            regret = turn_regret[a, :, lanes]
            weighted += regret * q
            weight += regret
            early = flop_regret[a : a + 1, lanes]
            top += early * flop_q
            bottom += early
        value = weighted / weight
        values[:, lanes] = value
        root = top / bottom
        for a in range(actions):
            q, flop_q = column(a * halves + half)
            turn_out[a, :, lanes] = jnp.maximum(turn_regret[a, :, lanes] + q - value, 0.0)
            early = flop_regret[a : a + 1, lanes]
            flop_out[a : a + 1, lanes] = jnp.maximum(early + flop_q - root, 0.0)


def shards(
    reach, ranks, live, turn_of, hand_cards, pot, turn_act, flop_act, turn_regret, flop_regret
):
    boards, seqs, width = reach.shape
    total_hands = hand_cards.shape[1]
    turns, actions, _ = turn_regret.shape
    rows = 2 * actions * boards
    boards_all = boards * lax.axis_size("turn")
    params = pltpu.CompilerParams(vmem_limit_bytes=VMEM)
    f32 = jnp.float32

    operands = (pot, turn_act, flop_act, turn_of, jnp.transpose(reach, (1, 0, 2)), ranks, live)
    payload = pl.pallas_call(
        weigh,
        out_shape=jax.ShapeDtypeStruct((width // 128, rows + 2 * boards, 128), f32),
        in_specs=[pl.BlockSpec(memory_space=pltpu.HBM)] * 7,
        out_specs=pl.BlockSpec(memory_space=pltpu.VMEM),
        scratch_shapes=[
            pltpu.SMEM(pot.shape, f32),
            pltpu.SMEM(turn_act.shape, jnp.int32),
            pltpu.SMEM(flop_act.shape, jnp.int32),
            pltpu.SMEM(turn_of.shape, jnp.int32),
            pltpu.VMEM((seqs, boards, width), reach.dtype),
            pltpu.VMEM(ranks.shape, jnp.int32),
            pltpu.VMEM(live.shape, jnp.int32),
            pltpu.SemaphoreType.DMA((7,)),
            *[pltpu.VMEM((actions, boards, width), f32)] * (2 * BANKS),
        ],
        compiler_params=params,
    )(*[pltpu.with_memory_space_constraint(x, pltpu.HBM) for x in operands])

    gathered = lax.all_gather(payload, "hand", axis=0, tiled=False)

    sums = pl.pallas_call(
        showdown,
        out_shape=jax.ShapeDtypeStruct((PLANE, CHUNK, 128), jnp.int16),
        in_specs=spread(4),
        out_specs=pl.BlockSpec(memory_space=pltpu.VMEM),
        scratch_shapes=[
            pltpu.VMEM((UNITS * 8, 128), f32),
        ],
        compiler_params=params,
    )(gathered, ranks, live, hand_cards)

    planes = [[k * LINE + z for k in range(PLANE)] for z in range(LINE)]
    lines = [[k * LINE + z for z in range(LINE)] for k in range(PLANE)]

    def copies(blocks, count):
        return pl.pallas_call(
            add_up,
            out_shape=jax.ShapeDtypeStruct((count, CHUNK, 128), jnp.int16),
            in_specs=spread(1),
            out_specs=pl.BlockSpec(memory_space=pltpu.VMEM),
            compiler_params=params,
        )(blocks)

    def swap(blocks, groups):
        return lax.all_to_all(blocks, "turn", 0, 0, axis_index_groups=groups, tiled=True)

    blocks = swap(sums, planes)
    blocks = swap(copies(blocks, LINE), lines)
    blocks = swap(copies(blocks, PLANE), planes)

    def last(*refs):
        settle(
            turns / boards_all / total_hands, 1.0 / boards_all / total_hands, *refs
        )

    turn_out, flop_out, values = pl.pallas_call(
        last,
        out_shape=(
            jax.ShapeDtypeStruct((actions, turns, width), f32),
            jax.ShapeDtypeStruct((actions, width), f32),
            jax.ShapeDtypeStruct((turns, width), f32),
        ),
        in_specs=spread(3),
        out_specs=tuple(spread(3)),
        scratch_shapes=[pltpu.VMEM((UNITS * 8, 128), f32)],
        compiler_params=params,
    )(blocks, jnp.transpose(turn_regret, (1, 0, 2)), flop_regret)
    return (jnp.transpose(turn_out, (1, 0, 2)), flop_out, values)


def solution(mesh):
    return jax.shard_map(
        shards,
        mesh=mesh,
        in_specs=(
            P("turn", None, "hand"),
            P("turn", "hand"),
            P("turn", "hand"),
            P("turn"),
            P(),
            P(),
            P(),
            P(),
            P(None, None, "hand"),
            P(None, "hand"),
        ),
        out_specs=(P(None, None, "hand"), P(None, "hand"), P(None, "hand")),
        check_vma=False,
    )
```

```python
import jax
import jax.numpy as jnp
from jax import lax
from jax.experimental import pallas as pl
from jax.experimental.pallas import tpu as pltpu
from jax.sharding import PartitionSpec as P

TURNS = 49
SLOTS = 56
UNITS = 128
PLANE = 16
LINE = 8
CHUNK = UNITS * 8 // PLANE
STEPS = 32760.0
SCALES = 58
BOARD_ROWS = 96
BOARD_SCALES = 90
PAGE = 8
FLOPS = 144
PAGE_SCALES = 162
PAGE_ROWS = 176
SPAN = 64
VMEM = 48 * 1024 * 1024
BANKS = 4


def spread(count):
    return [pl.BlockSpec(memory_space=pltpu.VMEM)] * count


def place(column, tile):
    columns, tiles = UNITS // (SLOTS // 8), SLOTS // 8
    if tile == tiles - 1 and column < PLANE:
        return column * CHUNK + CHUNK - 8
    spot = column * (tiles - 1) + tile if tile < tiles - 1 else columns * (tiles - 1) + column - PLANE
    return spot // 7 * CHUNK + spot % 7 * 8


def encode(x):
    top = jnp.maximum(jnp.max(jnp.abs(x), axis=1, keepdims=True), 1e-30)
    log = jnp.ceil(jnp.log2(top) * 256.0)
    return jnp.round(x * (STEPS / jnp.exp2(log * (1.0 / 256.0)))), log


def pack(x):
    row = lax.broadcasted_iota(jnp.int32, x.shape, 0)
    lane = lax.broadcasted_iota(jnp.int32, x.shape, 1)
    codes, log = encode(x)
    logs = jnp.sum(jnp.where(row == lane, log, 0.0), axis=0, keepdims=True)
    return jnp.where(row == SCALES, logs, codes).astype(jnp.int32).astype(jnp.int16)


def unpack(blocks):
    count = blocks.shape[0]
    ends = [blocks[k, 48:64, :].astype(jnp.int32).astype(jnp.float32) for k in range(count)]
    logs = jnp.concatenate([end[SCALES - 48 : SCALES - 47] for end in ends], axis=0)
    scales = jnp.transpose(jnp.exp2(logs * (1.0 / 256.0)) * (1.0 / STEPS))
    for k in range(count):
        codes = blocks[k].astype(jnp.int32).astype(jnp.float32)
        yield codes * scales[:64, k : k + 1]


def weigh(
    pot_hbm, turn_hbm, flop_hbm, of_hbm, reach_hbm, ranks_hbm, live_hbm, out,
    pot, turn_act, flop_act, turn_of, reach, ranks, live, sems, *banks
):
    pairs = (
        (reach_hbm, reach), (pot_hbm, pot), (turn_hbm, turn_act), (flop_hbm, flop_act),
        (of_hbm, turn_of), (ranks_hbm, ranks), (live_hbm, live),
    )
    moves = [pltpu.make_async_copy(x, y, sems.at[k]) for k, (x, y) in enumerate(pairs)]
    for move in moves:
        move.start()
    turn_sums, flop_sums = banks[:BANKS], banks[BANKS:]
    for bank in banks:
        bank[...] = jnp.zeros_like(bank)
    for move in moves:
        move.wait()
    seqs, boards, width = reach.shape
    halves = [slice(half * 128, half * 128 + 128) for half in range(width // 128)]
    for s in range(seqs):
        term = reach[s].astype(jnp.float32) * pot[s]
        turn_sums[s % BANKS][turn_act[s]] += term
        flop_sums[s % BANKS][flop_act[s]] += term
    alive = live[...].astype(jnp.float32)
    top = 0
    for sums in (turn_sums, flop_sums):
        for r in range(sums[0].shape[0]):
            total = sums[0][r]
            for other in sums[1:]:
                total += other[r]
            total *= alive
            for half, lanes in enumerate(halves):
                out[half, pl.ds(top, boards), :] = total[:, lanes]
            top += boards
    for half, lanes in enumerate(halves):
        out[half, pl.ds(top, boards), :] = ranks[:, lanes].astype(jnp.float32)
        for b in range(boards):
            card = jnp.full((1, 128), turn_of[b], jnp.int32).astype(jnp.float32)
            out[half, pl.ds(top + boards + b, 1), :] = card


def board_values(payload, ranks, live, cards):
    hands, halves, rows, _ = payload.shape
    width = halves * 128
    boards = ranks.shape[0]
    each = rows // boards
    me = lax.axis_index("hand")
    here = cards[:, pl.ds(pl.multiple_of(me * width, width), width)].astype(jnp.float32)
    mine = jnp.concatenate(
        [ranks[...].astype(jnp.float32), here, jnp.zeros((2, width), jnp.float32)], axis=0
    )
    columns = jnp.transpose(mine)
    first, second = columns[:, boards : boards + 1], columns[:, boards + 1 : boards + 2]
    aparts = []
    for h in range(hands):
        there = cards[:, h * width : (h + 1) * width].astype(jnp.float32)
        one, two = there[0:1], there[1:2]
        shared = (first == one) | (first == two) | (second == one) | (second == two)
        aparts.append(jnp.where(shared, 0.0, 1.0))
    apart = jnp.concatenate(aparts, axis=1)
    tall = -(-each // 8) * 8
    sums, turn_cards = [], []
    for b in range(boards):
        x = jnp.concatenate(
            [payload[h, half, pl.ds(b, each, stride=boards), :] for h in range(hands) for half in range(halves)],
            axis=1,
        )
        theirs = x[each - 2 : each - 1]
        turn_cards.append(x[each - 1 : each, :128])
        x = jnp.concatenate([x, jnp.zeros((tall - each, hands * width), jnp.float32)], axis=0)
        high = x.astype(jnp.bfloat16).astype(jnp.float32)
        mid = (x - high).astype(jnp.bfloat16).astype(jnp.float32)
        pieces = jnp.concatenate([high, mid, x - high - mid], axis=0).astype(jnp.bfloat16)
        sign = jnp.clip(columns[:, b : b + 1] - theirs, -1.0, 1.0)
        tile = (sign * apart).astype(jnp.bfloat16)
        part = lax.dot_general(
            pieces, tile, (((1,), (1,)), ((), ())), preferred_element_type=jnp.float32
        )
        part = part[:tall] + (part[tall : 2 * tall] + part[2 * tall :])
        sums.append(part * live[b : b + 1, :].astype(jnp.float32))
    return sums, turn_cards, (each - 2) // 2


def showdown_all(payload, ranks, live, cards, out, dense):
    sums, turn_cards, actions = board_values(payload, ranks, live, cards)
    width = sums[0].shape[1]
    flops = sums[0]
    for part in sums[1:]:
        flops += part
    slot = lax.broadcasted_iota(jnp.int32, (SLOTS, 128), 0)
    hits = [(slot.astype(jnp.float32) == card).astype(jnp.float32) for card in turn_cards]
    flop = (slot == TURNS).astype(jnp.float32)
    for a in range(actions):
        for half in range(width // 128):
            lanes = slice(half * 128, half * 128 + 128)
            block = flop * flops[actions + a : actions + a + 1, lanes]
            for hit, part in zip(hits, sums):
                block += hit * part[a : a + 1, lanes]
            column = a * (width // 128) + half
            for tile in range(SLOTS // 8):
                dense[pl.ds(place(column, tile), 8), :] = block[tile * 8 : tile * 8 + 8]
    spots = {place(c, t) for c in range(actions * (width // 128)) for t in range(SLOTS // 8)}
    for spot in sorted(set(range(0, UNITS * 8, 8)) - spots):
        dense[pl.ds(spot, 8), :] = jnp.zeros((8, 128), jnp.float32)
    for k in range(PLANE):
        out[k] = pack(dense[pl.ds(k * CHUNK, CHUNK), :])


def showdown(payload, ranks, live, cards, out, rows):
    sums, turn_cards, actions = board_values(payload, ranks, live, cards)
    halves = sums[0].shape[1] // 128
    flops = sums[0]
    for part in sums[1:]:
        flops += part
    rows[...] = jnp.zeros_like(rows)
    for b, part in enumerate(sums):
        for half in range(halves):
            lanes = slice(half * 128, half * 128 + 128)
            rows[pl.ds((b * halves + half) * actions, actions), :] = part[:actions, lanes]
    for half in range(halves):
        lanes = slice(half * 128, half * 128 + 128)
        at = (len(sums) * halves + half) * actions
        rows[pl.ds(at, actions), :] = flops[actions : 2 * actions, lanes]
    x = rows[...]
    row = lax.broadcasted_iota(jnp.int32, x.shape, 0)
    lane = lax.broadcasted_iota(jnp.int32, x.shape, 1)
    codes, log = encode(x)
    logs = jnp.sum(jnp.where(row == lane, log, 0.0), axis=0, keepdims=True)
    ids = jnp.zeros((1, 128), jnp.float32)
    for b, card in enumerate(turn_cards):
        ids = jnp.where(lane[:1] == b, card, ids)
    codes = jnp.where(row == BOARD_SCALES, logs, codes)
    codes = jnp.where(row == BOARD_SCALES + 1, ids, codes)
    codes = codes.astype(jnp.int32).astype(jnp.int16)
    for k in range(out.shape[0]):
        out[k] = codes


def run_sums(blocks, out, rows, page):
    count = blocks.shape[0]
    boards, halves, actions = 4, 2, 9
    tails = [blocks[k, 80:96, :].astype(jnp.int32).astype(jnp.float32) for k in range(count)]
    at = BOARD_SCALES - 80
    logs = jnp.concatenate([tail[at : at + 1] for tail in tails], axis=0)
    scales = jnp.transpose(jnp.exp2(logs * (1.0 / 256.0)) * (1.0 / STEPS))
    for k in range(count):
        codes = blocks[k].astype(jnp.int32).astype(jnp.float32)
        rows[k] = codes * scales[:96, k : k + 1]
    ids = [tail[at + 1 : at + 2] for tail in tails]
    least = ids[0][:, 0:1]
    most = ids[-1][:, boards - 1 : boards]
    slot = lax.broadcasted_iota(jnp.int32, (PAGE, 128), 0).astype(jnp.float32)
    hits = [
        [(slot == ids[k][:, b : b + 1] - least).astype(jnp.float32) for b in range(boards)]
        for k in range(count)
    ]
    page[...] = jnp.zeros_like(page)
    for a in range(actions):
        for half in range(halves):
            block = jnp.zeros((PAGE, 128), jnp.float32)
            for k in range(count):
                for b in range(boards):
                    block += hits[k][b] * rows[k, pl.ds((b * halves + half) * actions + a, 1), :]
            page[pl.ds((a * halves + half) * PAGE, PAGE), :] = block
    top, flops = boards * halves * actions, halves * actions
    total = rows[0, pl.ds(top, flops), :]
    for k in range(1, count):
        total += rows[k, pl.ds(top, flops), :]
    page[pl.ds(FLOPS, flops), :] = total
    x = page[...]
    row = lax.broadcasted_iota(jnp.int32, x.shape, 0)
    lane = lax.broadcasted_iota(jnp.int32, x.shape, 1)
    codes, log = encode(x)
    for part in range(2):
        logs = jnp.sum(jnp.where(row == lane + 128 * part, log, 0.0), axis=0, keepdims=True)
        codes = jnp.where(row == PAGE_SCALES + part, logs, codes)
    codes = jnp.where(row == PAGE_SCALES + 2, least, codes)
    codes = jnp.where(row == PAGE_SCALES + 3, most - least + 1.0, codes)
    codes = codes.astype(jnp.int32).astype(jnp.int16)
    for k in range(out.shape[0]):
        out[k] = codes


def finish(turns_over_boards, over_boards, blocks, turn_regret, flop_regret, turn_out, flop_out, values, cards, dense):
    actions, turns, width = turn_regret.shape
    halves, count = width // 128, blocks.shape[0]
    at = PAGE_SCALES - 160
    tails = [blocks[k, 160:176, :].astype(jnp.int32).astype(jnp.float32) for k in range(count)]
    scales = [
        jnp.transpose(
            jnp.exp2(jnp.concatenate([tail[at + part : at + part + 1] for tail in tails], axis=0) * (1.0 / 256.0))
            * (1.0 / STEPS)
        )
        for part in range(2)
    ]
    held = jnp.concatenate([tail[at + 3 : at + 4] for tail in tails], axis=0)
    cards[0] = jnp.max(held).astype(jnp.int32)
    dense[...] = jnp.zeros_like(dense)
    flops = jnp.zeros((32, 128), jnp.float32)
    for k in range(count):
        codes = blocks[k].astype(jnp.int32).astype(jnp.float32)
        early = codes[:128] * scales[0][:, k : k + 1]
        late = codes[128:] * scales[1][:48, k : k + 1]
        flops += late[16:48]
        least = jnp.max(tails[k][at + 2 : at + 3]).astype(jnp.int32)
        for column in range(actions * halves):
            start = column * PAGE
            tile = early[start : start + PAGE] if start < 128 else late[start - 128 : start - 128 + PAGE]
            dense[pl.ds(column * SPAN + least, PAGE), :] += tile
    for half in range(halves):
        lanes = pl.ds(half * 128, 128)
        weighted = jnp.zeros((turns, 128), jnp.float32)
        weight = jnp.zeros((turns, 128), jnp.float32)
        for a in range(actions):
            q = dense[pl.ds((a * halves + half) * SPAN, turns), :] * turns_over_boards
            regret = turn_regret[a, :, lanes]
            weighted += regret * q
            weight += regret
        value = weighted / weight
        values[:, lanes] = value
        early = flop_regret[:, lanes]
        flop_q = flops[half * actions : half * actions + actions] * over_boards
        root = jnp.sum(early * flop_q, axis=0, keepdims=True) / jnp.sum(early, axis=0, keepdims=True)
        flop_out[:, lanes] = jnp.maximum(early + flop_q - root, 0.0)
        for a in range(actions):
            q = dense[pl.ds((a * halves + half) * SPAN, turns), :] * turns_over_boards
            turn_out[a, :, lanes] = jnp.maximum(turn_regret[a, :, lanes] + q - value, 0.0)


def add_up(blocks, out):
    total = jnp.zeros((CHUNK, 128), jnp.float32)
    for block in unpack(blocks):
        total += block
    row = lax.broadcasted_iota(jnp.int32, total.shape, 0)
    codes = pack(jnp.where(row == SCALES, 0.0, total))
    for k in range(out.shape[0]):
        out[k] = codes


def settle(turns_over_boards, over_boards, blocks, turn_regret, flop_regret, turn_out, flop_out, values, sums):
    actions, turns, width = turn_regret.shape
    halves = width // 128
    for k, block in enumerate(unpack(blocks)):
        sums[pl.ds(k * CHUNK, CHUNK), :] = block

    def column(at):
        tiles = [sums[pl.ds(place(at, tile), 8), :] for tile in range(SLOTS // 8)]
        whole = jnp.concatenate(tiles, axis=0)
        return whole[:turns] * turns_over_boards, whole[turns : turns + 1] * over_boards

    for half in range(halves):
        lanes = pl.ds(half * 128, 128)
        weighted = jnp.zeros((turns, 128), jnp.float32)
        weight = jnp.zeros((turns, 128), jnp.float32)
        top = jnp.zeros((1, 128), jnp.float32)
        bottom = jnp.zeros((1, 128), jnp.float32)
        for a in range(actions):
            q, flop_q = column(a * halves + half)
            regret = turn_regret[a, :, lanes]
            weighted += regret * q
            weight += regret
            early = flop_regret[a : a + 1, lanes]
            top += early * flop_q
            bottom += early
        value = weighted / weight
        values[:, lanes] = value
        root = top / bottom
        for a in range(actions):
            q, flop_q = column(a * halves + half)
            turn_out[a, :, lanes] = jnp.maximum(turn_regret[a, :, lanes] + q - value, 0.0)
            early = flop_regret[a : a + 1, lanes]
            flop_out[a : a + 1, lanes] = jnp.maximum(early + flop_q - root, 0.0)


def shards(
    reach, ranks, live, turn_of, hand_cards, pot, turn_act, flop_act, turn_regret, flop_regret
):
    boards, seqs, width = reach.shape
    total_hands = hand_cards.shape[1]
    turns, actions, _ = turn_regret.shape
    rows = 2 * actions * boards
    boards_all = boards * lax.axis_size("turn")
    params = pltpu.CompilerParams(vmem_limit_bytes=VMEM)
    f32 = jnp.float32

    operands = (pot, turn_act, flop_act, turn_of, jnp.transpose(reach, (1, 0, 2)), ranks, live)
    payload = pl.pallas_call(
        weigh,
        out_shape=jax.ShapeDtypeStruct((width // 128, rows + 2 * boards, 128), f32),
        in_specs=[pl.BlockSpec(memory_space=pltpu.HBM)] * 7,
        out_specs=pl.BlockSpec(memory_space=pltpu.VMEM),
        scratch_shapes=[
            pltpu.SMEM(pot.shape, f32),
            pltpu.SMEM(turn_act.shape, jnp.int32),
            pltpu.SMEM(flop_act.shape, jnp.int32),
            pltpu.SMEM(turn_of.shape, jnp.int32),
            pltpu.VMEM((seqs, boards, width), reach.dtype),
            pltpu.VMEM(ranks.shape, jnp.int32),
            pltpu.VMEM(live.shape, jnp.int32),
            pltpu.SemaphoreType.DMA((7,)),
            *[pltpu.VMEM((actions, boards, width), f32)] * (2 * BANKS),
        ],
        compiler_params=params,
    )(*[pltpu.with_memory_space_constraint(x, pltpu.HBM) for x in operands])

    gathered = lax.all_gather(payload, "hand", axis=0, tiled=False)

    planes = [[k * LINE + z for k in range(PLANE)] for z in range(LINE)]
    lines = [[k * LINE + z for z in range(LINE)] for k in range(PLANE)]
    vmem = pl.BlockSpec(memory_space=pltpu.VMEM)
    factors = (turns / boards_all / total_hands, 1.0 / boards_all / total_hands)
    by_action = jnp.transpose(turn_regret, (1, 0, 2))
    outputs = (
        jax.ShapeDtypeStruct((actions, turns, width), f32),
        jax.ShapeDtypeStruct((actions, width), f32),
        jax.ShapeDtypeStruct((turns, width), f32),
    )

    def call(kernel, shape, scratch, *args):
        return pl.pallas_call(
            kernel,
            out_shape=jax.ShapeDtypeStruct(shape, jnp.int16),
            in_specs=spread(len(args)),
            out_specs=vmem,
            scratch_shapes=[pltpu.VMEM(dims, f32) for dims in scratch],
            compiler_params=params,
        )(*args)

    def swap(blocks, groups):
        return lax.all_to_all(blocks, "turn", 0, 0, axis_index_groups=groups, tiled=True)

    blocks = call(
        showdown, (LINE, BOARD_ROWS, 128), [(BOARD_ROWS, 128)], gathered, ranks, live, hand_cards
    )
    blocks = swap(blocks, lines)
    blocks = call(
        run_sums, (PLANE, PAGE_ROWS, 128), [(LINE, BOARD_ROWS, 128), (PAGE_ROWS, 128)], blocks
    )
    blocks = swap(blocks, planes)
    turn_out, flop_out, values, cards = pl.pallas_call(
        lambda *refs: finish(*factors, *refs),
        out_shape=outputs + (jax.ShapeDtypeStruct((1,), jnp.int32),),
        in_specs=spread(3),
        out_specs=tuple(spread(3)) + (pl.BlockSpec(memory_space=pltpu.SMEM),),
        scratch_shapes=[pltpu.VMEM((actions * (width // 128) * SPAN, 128), f32)],
        compiler_params=params,
    )(blocks, by_action, flop_regret)

    def every_card(state):
        payload = gathered + jnp.where(state[0] > PAGE, 0.0, 1.0)
        scratch = [(UNITS * 8, 128)]
        chunks = call(
            showdown_all, (PLANE, CHUNK, 128), scratch, payload, ranks, live, hand_cards
        )
        chunks = swap(chunks, planes)
        chunks = swap(call(add_up, (LINE, CHUNK, 128), [], chunks), lines)
        chunks = swap(call(add_up, (PLANE, CHUNK, 128), [], chunks), planes)
        results = pl.pallas_call(
            lambda *refs: settle(*factors, *refs),
            out_shape=outputs,
            in_specs=spread(3),
            out_specs=tuple(spread(3)),
            scratch_shapes=[pltpu.VMEM((UNITS * 8, 128), f32)],
            compiler_params=params,
        )(chunks, by_action, flop_regret)
        return (jnp.int32(0),) + tuple(results)

    state = (cards[0], turn_out, flop_out, values)
    _, turn_out, flop_out, values = lax.while_loop(lambda s: s[0] > PAGE, every_card, state)
    return (jnp.transpose(turn_out, (1, 0, 2)), flop_out, values)


def solution(mesh):
    return jax.shard_map(
        shards,
        mesh=mesh,
        in_specs=(
            P("turn", None, "hand"),
            P("turn", "hand"),
            P("turn", "hand"),
            P("turn"),
            P(),
            P(),
            P(),
            P(),
            P(None, None, "hand"),
            P(None, "hand"),
        ),
        out_specs=(P(None, None, "hand"), P(None, "hand"), P(None, "hand")),
        check_vma=False,
    )
```

```python
import jax
import jax.numpy as jnp
from jax import lax
from jax.experimental import pallas as pl
from jax.experimental.pallas import tpu as pltpu
from jax.sharding import PartitionSpec as P

TURNS = 49
SLOTS = 56
UNITS = 128
PLANE = 16
LINE = 8
CHUNK = UNITS * 8 // PLANE
STEPS = 32760.0
SCALES = 58
BOARD_ROWS = 96
BOARD_SCALES = 90
PAGE = 8
FLOPS = 144
PAGE_SCALES = 162
PAGE_ROWS = 176
SPAN = 64
VMEM = 48 * 1024 * 1024
BANKS = 4


def spread(count):
    return [pl.BlockSpec(memory_space=pltpu.VMEM)] * count


def place(column, tile):
    columns, tiles = UNITS // (SLOTS // 8), SLOTS // 8
    if tile == tiles - 1 and column < PLANE:
        return column * CHUNK + CHUNK - 8
    spot = column * (tiles - 1) + tile if tile < tiles - 1 else columns * (tiles - 1) + column - PLANE
    return spot // 7 * CHUNK + spot % 7 * 8


def encode(x):
    top = jnp.maximum(jnp.max(jnp.abs(x), axis=1, keepdims=True), 1e-30)
    log = jnp.ceil(jnp.log2(top) * 256.0)
    return jnp.round(x * (STEPS / jnp.exp2(log * (1.0 / 256.0)))), log


def pack(x):
    row = lax.broadcasted_iota(jnp.int32, x.shape, 0)
    lane = lax.broadcasted_iota(jnp.int32, x.shape, 1)
    codes, log = encode(x)
    logs = jnp.sum(jnp.where(row == lane, log, 0.0), axis=0, keepdims=True)
    return jnp.where(row == SCALES, logs, codes).astype(jnp.int32).astype(jnp.int16)


def unpack(blocks):
    count = blocks.shape[0]
    ends = [blocks[k, 48:64, :].astype(jnp.int32).astype(jnp.float32) for k in range(count)]
    logs = jnp.concatenate([end[SCALES - 48 : SCALES - 47] for end in ends], axis=0)
    scales = jnp.transpose(jnp.exp2(logs * (1.0 / 256.0)) * (1.0 / STEPS))
    for k in range(count):
        codes = blocks[k].astype(jnp.int32).astype(jnp.float32)
        yield codes * scales[:64, k : k + 1]


def weigh(
    pot_hbm, turn_hbm, flop_hbm, of_hbm, reach_hbm, ranks_hbm, live_hbm, out,
    pot, turn_act, flop_act, turn_of, reach, ranks, live, sems, *banks
):
    pairs = (
        (reach_hbm, reach), (pot_hbm, pot), (turn_hbm, turn_act), (flop_hbm, flop_act),
        (of_hbm, turn_of), (ranks_hbm, ranks), (live_hbm, live),
    )
    moves = [pltpu.make_async_copy(x, y, sems.at[k]) for k, (x, y) in enumerate(pairs)]
    for move in moves:
        move.start()
    turn_sums, flop_sums = banks[:BANKS], banks[BANKS:]
    for bank in banks:
        bank[...] = jnp.zeros_like(bank)
    for move in moves:
        move.wait()
    seqs, boards, width = reach.shape
    halves = [slice(half * 128, half * 128 + 128) for half in range(width // 128)]
    for s in range(seqs):
        term = reach[s].astype(jnp.float32) * pot[s]
        turn_sums[s % BANKS][turn_act[s]] += term
        flop_sums[s % BANKS][flop_act[s]] += term
    alive = live[...].astype(jnp.float32)
    top = 0
    for sums in (turn_sums, flop_sums):
        for r in range(sums[0].shape[0]):
            total = sums[0][r]
            for other in sums[1:]:
                total += other[r]
            total *= alive
            for half, lanes in enumerate(halves):
                out[half, pl.ds(top, boards), :] = total[:, lanes]
            top += boards
    for half, lanes in enumerate(halves):
        out[half, pl.ds(top, boards), :] = ranks[:, lanes].astype(jnp.float32)
        for b in range(boards):
            card = jnp.full((1, 128), turn_of[b], jnp.int32).astype(jnp.float32)
            out[half, pl.ds(top + boards + b, 1), :] = card


def board_values(payload, ranks, live, cards):
    hands, halves, rows, _ = payload.shape
    width = halves * 128
    boards = ranks.shape[0]
    each = rows // boards
    me = lax.axis_index("hand")
    here = cards[:, pl.ds(pl.multiple_of(me * width, width), width)].astype(jnp.float32)
    mine = jnp.concatenate(
        [ranks[...].astype(jnp.float32), here, jnp.zeros((2, width), jnp.float32)], axis=0
    )
    columns = jnp.transpose(mine)
    first, second = columns[:, boards : boards + 1], columns[:, boards + 1 : boards + 2]
    aparts = []
    for h in range(hands):
        there = cards[:, h * width : (h + 1) * width].astype(jnp.float32)
        one, two = there[0:1], there[1:2]
        shared = (first == one) | (first == two) | (second == one) | (second == two)
        aparts.append(jnp.where(shared, 0.0, 1.0))
    apart = jnp.concatenate(aparts, axis=1)
    tall = -(-each // 8) * 8
    sums, turn_cards = [], []
    for b in range(boards):
        x = jnp.concatenate(
            [payload[h, half, pl.ds(b, each, stride=boards), :] for h in range(hands) for half in range(halves)],
            axis=1,
        )
        theirs = x[each - 2 : each - 1]
        turn_cards.append(x[each - 1 : each, :128])
        x = jnp.concatenate([x, jnp.zeros((tall - each, hands * width), jnp.float32)], axis=0)
        high = x.astype(jnp.bfloat16).astype(jnp.float32)
        mid = (x - high).astype(jnp.bfloat16).astype(jnp.float32)
        pieces = jnp.concatenate([high, mid, x - high - mid], axis=0).astype(jnp.bfloat16)
        sign = jnp.clip(columns[:, b : b + 1] - theirs, -1.0, 1.0)
        tile = (sign * apart).astype(jnp.bfloat16)
        part = lax.dot_general(
            pieces, tile, (((1,), (1,)), ((), ())), preferred_element_type=jnp.float32
        )
        part = part[:tall] + (part[tall : 2 * tall] + part[2 * tall :])
        sums.append(part * live[b : b + 1, :].astype(jnp.float32))
    return sums, turn_cards, (each - 2) // 2


def showdown_all(payload, ranks, live, cards, out, dense):
    sums, turn_cards, actions = board_values(payload, ranks, live, cards)
    width = sums[0].shape[1]
    flops = sums[0]
    for part in sums[1:]:
        flops += part
    slot = lax.broadcasted_iota(jnp.int32, (SLOTS, 128), 0)
    hits = [(slot.astype(jnp.float32) == card).astype(jnp.float32) for card in turn_cards]
    flop = (slot == TURNS).astype(jnp.float32)
    for a in range(actions):
        for half in range(width // 128):
            lanes = slice(half * 128, half * 128 + 128)
            block = flop * flops[actions + a : actions + a + 1, lanes]
            for hit, part in zip(hits, sums):
                block += hit * part[a : a + 1, lanes]
            column = a * (width // 128) + half
            for tile in range(SLOTS // 8):
                dense[pl.ds(place(column, tile), 8), :] = block[tile * 8 : tile * 8 + 8]
    spots = {place(c, t) for c in range(actions * (width // 128)) for t in range(SLOTS // 8)}
    for spot in sorted(set(range(0, UNITS * 8, 8)) - spots):
        dense[pl.ds(spot, 8), :] = jnp.zeros((8, 128), jnp.float32)
    for k in range(PLANE):
        out[k] = pack(dense[pl.ds(k * CHUNK, CHUNK), :])


def showdown(payload, ranks, live, cards, out, rows):
    sums, turn_cards, actions = board_values(payload, ranks, live, cards)
    halves = sums[0].shape[1] // 128
    flops = sums[0]
    for part in sums[1:]:
        flops += part
    rows[...] = jnp.zeros_like(rows)
    for b, part in enumerate(sums):
        for half in range(halves):
            lanes = slice(half * 128, half * 128 + 128)
            rows[pl.ds((b * halves + half) * actions, actions), :] = part[:actions, lanes]
    for half in range(halves):
        lanes = slice(half * 128, half * 128 + 128)
        at = (len(sums) * halves + half) * actions
        rows[pl.ds(at, actions), :] = flops[actions : 2 * actions, lanes]
    x = rows[...]
    row = lax.broadcasted_iota(jnp.int32, x.shape, 0)
    lane = lax.broadcasted_iota(jnp.int32, x.shape, 1)
    codes, log = encode(x)
    logs = jnp.sum(jnp.where(row == lane, log, 0.0), axis=0, keepdims=True)
    ids = jnp.zeros((1, 128), jnp.float32)
    for b, card in enumerate(turn_cards):
        ids = jnp.where(lane[:1] == b, card, ids)
    codes = jnp.where(row == BOARD_SCALES, logs, codes)
    codes = jnp.where(row == BOARD_SCALES + 1, ids, codes)
    codes = codes.astype(jnp.int32).astype(jnp.int16)
    for k in range(out.shape[0]):
        out[k] = codes


def run_sums(blocks, out, rows, page):
    count = blocks.shape[0]
    boards, halves, actions = 4, 2, 9
    tails = [blocks[k, 80:96, :].astype(jnp.int32).astype(jnp.float32) for k in range(count)]
    at = BOARD_SCALES - 80
    logs = jnp.concatenate([tail[at : at + 1] for tail in tails], axis=0)
    scales = jnp.transpose(jnp.exp2(logs * (1.0 / 256.0)) * (1.0 / STEPS))
    for k in range(count):
        codes = blocks[k].astype(jnp.int32).astype(jnp.float32)
        rows[k] = codes * scales[:96, k : k + 1]
    ids = [tail[at + 1 : at + 2] for tail in tails]
    least = ids[0][:, 0:1]
    most = ids[-1][:, boards - 1 : boards]
    slot = lax.broadcasted_iota(jnp.int32, (PAGE, 128), 0).astype(jnp.float32)
    hits = [
        [(slot == ids[k][:, b : b + 1] - least).astype(jnp.float32) for b in range(boards)]
        for k in range(count)
    ]
    page[...] = jnp.zeros_like(page)
    for a in range(actions):
        for half in range(halves):
            block = jnp.zeros((PAGE, 128), jnp.float32)
            for k in range(count):
                for b in range(boards):
                    block += hits[k][b] * rows[k, pl.ds((b * halves + half) * actions + a, 1), :]
            page[pl.ds((a * halves + half) * PAGE, PAGE), :] = block
    top, flops = boards * halves * actions, halves * actions
    total = rows[0, pl.ds(top, flops), :]
    for k in range(1, count):
        total += rows[k, pl.ds(top, flops), :]
    page[pl.ds(FLOPS, flops), :] = total
    x = page[...]
    row = lax.broadcasted_iota(jnp.int32, x.shape, 0)
    lane = lax.broadcasted_iota(jnp.int32, x.shape, 1)
    codes, log = encode(x)
    for part in range(2):
        logs = jnp.sum(jnp.where(row == lane + 128 * part, log, 0.0), axis=0, keepdims=True)
        codes = jnp.where(row == PAGE_SCALES + part, logs, codes)
    codes = jnp.where(row == PAGE_SCALES + 2, least, codes)
    codes = jnp.where(row == PAGE_SCALES + 3, most - least + 1.0, codes)
    codes = codes.astype(jnp.int32).astype(jnp.int16)
    for k in range(out.shape[0]):
        out[k] = codes


def finish(turns_over_boards, over_boards, blocks, turn_regret, flop_regret, turn_out, flop_out, values, cards, dense):
    actions, turns, width = turn_regret.shape
    halves, count = width // 128, blocks.shape[0]
    at = PAGE_SCALES - 160
    tails = [blocks[k, 160:176, :].astype(jnp.int32).astype(jnp.float32) for k in range(count)]
    scales = [
        jnp.transpose(
            jnp.exp2(jnp.concatenate([tail[at + part : at + part + 1] for tail in tails], axis=0) * (1.0 / 256.0))
            * (1.0 / STEPS)
        )
        for part in range(2)
    ]
    held = jnp.concatenate([tail[at + 3 : at + 4] for tail in tails], axis=0)
    cards[0] = jnp.max(held).astype(jnp.int32)
    leasts = [jnp.max(tail[at + 2 : at + 3]).astype(jnp.int32) for tail in tails]
    dense[...] = jnp.zeros_like(dense)
    flops = jnp.zeros((32, 128), jnp.float32)
    for k in range(count):
        codes = blocks[k].astype(jnp.int32).astype(jnp.float32)
        early = codes[:128] * scales[0][:, k : k + 1]
        late = codes[128:] * scales[1][:48, k : k + 1]
        flops += late[16:48]
        least = leasts[k]
        for column in range(actions * halves):
            start = column * PAGE
            tile = early[start : start + PAGE] if start < 128 else late[start - 128 : start - 128 + PAGE]
            dense[pl.ds(column * SPAN + least, PAGE), :] += tile
    for half in range(halves):
        lanes = pl.ds(half * 128, 128)
        weighted = jnp.zeros((turns, 128), jnp.float32)
        weight = jnp.zeros((turns, 128), jnp.float32)
        for a in range(actions):
            q = dense[pl.ds((a * halves + half) * SPAN, turns), :] * turns_over_boards
            regret = turn_regret[a, :, lanes]
            weighted += regret * q
            weight += regret
        value = weighted / weight
        values[:, lanes] = value
        early = flop_regret[:, lanes]
        flop_q = flops[half * actions : half * actions + actions] * over_boards
        root = jnp.sum(early * flop_q, axis=0, keepdims=True) / jnp.sum(early, axis=0, keepdims=True)
        flop_out[:, lanes] = jnp.maximum(early + flop_q - root, 0.0)
        for a in range(actions):
            q = dense[pl.ds((a * halves + half) * SPAN, turns), :] * turns_over_boards
            turn_out[a, :, lanes] = jnp.maximum(turn_regret[a, :, lanes] + q - value, 0.0)


def add_up(blocks, out):
    total = jnp.zeros((CHUNK, 128), jnp.float32)
    for block in unpack(blocks):
        total += block
    row = lax.broadcasted_iota(jnp.int32, total.shape, 0)
    codes = pack(jnp.where(row == SCALES, 0.0, total))
    for k in range(out.shape[0]):
        out[k] = codes


def settle(turns_over_boards, over_boards, blocks, turn_regret, flop_regret, turn_out, flop_out, values, sums):
    actions, turns, width = turn_regret.shape
    halves = width // 128
    for k, block in enumerate(unpack(blocks)):
        sums[pl.ds(k * CHUNK, CHUNK), :] = block

    def column(at):
        tiles = [sums[pl.ds(place(at, tile), 8), :] for tile in range(SLOTS // 8)]
        whole = jnp.concatenate(tiles, axis=0)
        return whole[:turns] * turns_over_boards, whole[turns : turns + 1] * over_boards

    for half in range(halves):
        lanes = pl.ds(half * 128, 128)
        weighted = jnp.zeros((turns, 128), jnp.float32)
        weight = jnp.zeros((turns, 128), jnp.float32)
        top = jnp.zeros((1, 128), jnp.float32)
        bottom = jnp.zeros((1, 128), jnp.float32)
        for a in range(actions):
            q, flop_q = column(a * halves + half)
            regret = turn_regret[a, :, lanes]
            weighted += regret * q
            weight += regret
            early = flop_regret[a : a + 1, lanes]
            top += early * flop_q
            bottom += early
        value = weighted / weight
        values[:, lanes] = value
        root = top / bottom
        for a in range(actions):
            q, flop_q = column(a * halves + half)
            turn_out[a, :, lanes] = jnp.maximum(turn_regret[a, :, lanes] + q - value, 0.0)
            early = flop_regret[a : a + 1, lanes]
            flop_out[a : a + 1, lanes] = jnp.maximum(early + flop_q - root, 0.0)


def shards(
    reach, ranks, live, turn_of, hand_cards, pot, turn_act, flop_act, turn_regret, flop_regret
):
    boards, seqs, width = reach.shape
    total_hands = hand_cards.shape[1]
    turns, actions, _ = turn_regret.shape
    rows = 2 * actions * boards
    boards_all = boards * lax.axis_size("turn")
    params = pltpu.CompilerParams(vmem_limit_bytes=VMEM)
    f32 = jnp.float32

    operands = (pot, turn_act, flop_act, turn_of, jnp.transpose(reach, (1, 0, 2)), ranks, live)
    payload = pl.pallas_call(
        weigh,
        out_shape=jax.ShapeDtypeStruct((width // 128, rows + 2 * boards, 128), f32),
        in_specs=[pl.BlockSpec(memory_space=pltpu.HBM)] * 7,
        out_specs=pl.BlockSpec(memory_space=pltpu.VMEM),
        scratch_shapes=[
            pltpu.SMEM(pot.shape, f32),
            pltpu.SMEM(turn_act.shape, jnp.int32),
            pltpu.SMEM(flop_act.shape, jnp.int32),
            pltpu.SMEM(turn_of.shape, jnp.int32),
            pltpu.VMEM((seqs, boards, width), reach.dtype),
            pltpu.VMEM(ranks.shape, jnp.int32),
            pltpu.VMEM(live.shape, jnp.int32),
            pltpu.SemaphoreType.DMA((7,)),
            *[pltpu.VMEM((actions, boards, width), f32)] * (2 * BANKS),
        ],
        compiler_params=params,
    )(*[pltpu.with_memory_space_constraint(x, pltpu.HBM) for x in operands])

    gathered = lax.all_gather(payload, "hand", axis=0, tiled=False)

    planes = [[k * LINE + z for k in range(PLANE)] for z in range(LINE)]
    lines = [[k * LINE + z for z in range(LINE)] for k in range(PLANE)]
    vmem = pl.BlockSpec(memory_space=pltpu.VMEM)
    factors = (turns / boards_all / total_hands, 1.0 / boards_all / total_hands)
    by_action = jnp.transpose(turn_regret, (1, 0, 2))
    outputs = (
        jax.ShapeDtypeStruct((actions, turns, width), f32),
        jax.ShapeDtypeStruct((actions, width), f32),
        jax.ShapeDtypeStruct((turns, width), f32),
    )

    def call(kernel, shape, scratch, *args):
        return pl.pallas_call(
            kernel,
            out_shape=jax.ShapeDtypeStruct(shape, jnp.int16),
            in_specs=spread(len(args)),
            out_specs=vmem,
            scratch_shapes=[pltpu.VMEM(dims, f32) for dims in scratch],
            compiler_params=params,
        )(*args)

    def swap(blocks, groups):
        return lax.all_to_all(blocks, "turn", 0, 0, axis_index_groups=groups, tiled=True)

    blocks = call(
        showdown, (LINE, BOARD_ROWS, 128), [(BOARD_ROWS, 128)], gathered, ranks, live, hand_cards
    )
    blocks = swap(blocks, lines)
    blocks = call(
        run_sums, (PLANE, PAGE_ROWS, 128), [(LINE, BOARD_ROWS, 128), (PAGE_ROWS, 128)], blocks
    )
    blocks = swap(blocks, planes)
    turn_out, flop_out, values, cards = pl.pallas_call(
        lambda *refs: finish(*factors, *refs),
        out_shape=outputs + (jax.ShapeDtypeStruct((1,), jnp.int32),),
        in_specs=spread(3),
        out_specs=tuple(spread(3)) + (pl.BlockSpec(memory_space=pltpu.SMEM),),
        scratch_shapes=[pltpu.VMEM((actions * (width // 128) * SPAN, 128), f32)],
        compiler_params=params,
    )(blocks, by_action, flop_regret)

    def every_card(state):
        payload = gathered + jnp.where(state[0] > PAGE, 0.0, 1.0)
        scratch = [(UNITS * 8, 128)]
        chunks = call(
            showdown_all, (PLANE, CHUNK, 128), scratch, payload, ranks, live, hand_cards
        )
        chunks = swap(chunks, planes)
        chunks = swap(call(add_up, (LINE, CHUNK, 128), [], chunks), lines)
        chunks = swap(call(add_up, (PLANE, CHUNK, 128), [], chunks), planes)
        results = pl.pallas_call(
            lambda *refs: settle(*factors, *refs),
            out_shape=outputs,
            in_specs=spread(3),
            out_specs=tuple(spread(3)),
            scratch_shapes=[pltpu.VMEM((UNITS * 8, 128), f32)],
            compiler_params=params,
        )(chunks, by_action, flop_regret)
        return (jnp.int32(0),) + tuple(results)

    state = (cards[0], turn_out, flop_out, values)
    _, turn_out, flop_out, values = lax.while_loop(lambda s: s[0] > PAGE, every_card, state)
    return (jnp.transpose(turn_out, (1, 0, 2)), flop_out, values)


def solution(mesh):
    return jax.shard_map(
        shards,
        mesh=mesh,
        in_specs=(
            P("turn", None, "hand"),
            P("turn", "hand"),
            P("turn", "hand"),
            P("turn"),
            P(),
            P(),
            P(),
            P(),
            P(None, None, "hand"),
            P(None, "hand"),
        ),
        out_specs=(P(None, None, "hand"), P(None, "hand"), P(None, "hand")),
        check_vma=False,
    )
```

```python
import jax
import jax.numpy as jnp
from jax import lax
from jax.experimental import pallas as pl
from jax.experimental.pallas import tpu as pltpu
from jax.sharding import PartitionSpec as P

TURNS = 49
SLOTS = 56
UNITS = 128
PLANE = 16
LINE = 8
CHUNK = UNITS * 8 // PLANE
STEPS = 32760.0
SCALES = 58
BOARD_ROWS = 96
BOARD_SCALES = 90
PAGE = 8
FLOPS = 144
PAGE_SCALES = 162
PAGE_ROWS = 176
SPAN = 64
VMEM = 48 * 1024 * 1024
BANKS = 4


def spread(count):
    return [pl.BlockSpec(memory_space=pltpu.VMEM)] * count


def place(column, tile):
    columns, tiles = UNITS // (SLOTS // 8), SLOTS // 8
    if tile == tiles - 1 and column < PLANE:
        return column * CHUNK + CHUNK - 8
    spot = column * (tiles - 1) + tile if tile < tiles - 1 else columns * (tiles - 1) + column - PLANE
    return spot // 7 * CHUNK + spot % 7 * 8


def encode(x):
    top = jnp.maximum(jnp.max(jnp.abs(x), axis=1, keepdims=True), 1e-30)
    log = jnp.ceil(jnp.log2(top) * 256.0)
    return jnp.round(x * (STEPS / jnp.exp2(log * (1.0 / 256.0)))), log


def pack(x):
    row = lax.broadcasted_iota(jnp.int32, x.shape, 0)
    lane = lax.broadcasted_iota(jnp.int32, x.shape, 1)
    codes, log = encode(x)
    logs = jnp.sum(jnp.where(row == lane, log, 0.0), axis=0, keepdims=True)
    return jnp.where(row == SCALES, logs, codes).astype(jnp.int32).astype(jnp.int16)


def unpack(blocks):
    count = blocks.shape[0]
    ends = [blocks[k, 48:64, :].astype(jnp.int32).astype(jnp.float32) for k in range(count)]
    logs = jnp.concatenate([end[SCALES - 48 : SCALES - 47] for end in ends], axis=0)
    scales = jnp.transpose(jnp.exp2(logs * (1.0 / 256.0)) * (1.0 / STEPS))
    for k in range(count):
        codes = blocks[k].astype(jnp.int32).astype(jnp.float32)
        yield codes * scales[:64, k : k + 1]


def row_tops(pot, turn_act, flop_act, count):
    row = lax.broadcasted_iota(jnp.int32, (24, pot.shape[1]), 0)
    key = jnp.where(row < count, turn_act[...], flop_act[...] + count)
    return jnp.sum(jnp.where(row == key, pot[...], 0.0), axis=1, keepdims=True)


def weigh(
    pot_hbm, turn_hbm, flop_hbm, of_hbm, reach_hbm, ranks_hbm, live_hbm, pots_hbm, turns_hbm, flops_hbm, out,
    pot, turn_act, flop_act, turn_of, reach, ranks, live, pots, turns, flops, stage, sems, *banks
):
    pairs = (
        (reach_hbm, reach), (pot_hbm, pot), (turn_hbm, turn_act), (flop_hbm, flop_act),
        (of_hbm, turn_of), (ranks_hbm, ranks), (live_hbm, live),
        (pots_hbm, pots), (turns_hbm, turns), (flops_hbm, flops),
    )
    moves = [pltpu.make_async_copy(x, y, sems.at[k]) for k, (x, y) in enumerate(pairs)]
    for move in moves:
        move.start()
    turn_sums, flop_sums = banks[:BANKS], banks[BANKS:]
    for bank in banks:
        bank[...] = jnp.zeros_like(bank)
    for move in moves:
        move.wait()
    seqs, boards, width = reach.shape
    halves = [slice(half * 128, half * 128 + 128) for half in range(width // 128)]
    for s in range(seqs):
        term = reach[s].astype(jnp.float32) * pot[s]
        turn_sums[s % BANKS][turn_act[s]] += term
        flop_sums[s % BANKS][flop_act[s]] += term
    alive = live[...].astype(jnp.float32)
    steps = 65535.0 / jnp.maximum(row_tops(pots, turns, flops, turn_sums[0].shape[0]), 1e-30)
    top = 0
    for sums in (turn_sums, flop_sums):
        for r in range(sums[0].shape[0]):
            total = sums[0][r]
            for other in sums[1:]:
                total += other[r]
            at = top // boards
            total = jnp.round(total * alive * steps[at : at + 1])
            total = jnp.minimum(total, 65535.0) - 32768.0
            for half, lanes in enumerate(halves):
                stage[half, pl.ds(top, boards), :] = total[:, lanes]
            top += boards
    for half, lanes in enumerate(halves):
        stage[half, pl.ds(top, boards), :] = ranks[:, lanes].astype(jnp.float32)
        for b in range(boards):
            card = jnp.full((1, 128), turn_of[b], jnp.int32).astype(jnp.float32)
            stage[half, pl.ds(top + boards + b, 1), :] = card
    out[...] = stage[...].astype(jnp.int32).astype(jnp.int16)


def board_values(payload, ranks, live, cards, pot, turn_act, flop_act, wide):
    hands, halves, rows, _ = payload.shape
    width = halves * 128
    boards = ranks.shape[0]
    each = rows // boards
    me = lax.axis_index("hand")
    here = cards[:, pl.ds(pl.multiple_of(me * width, width), width)].astype(jnp.float32)
    mine = jnp.concatenate(
        [ranks[...].astype(jnp.float32), here, jnp.zeros((2, width), jnp.float32)], axis=0
    )
    columns = jnp.transpose(mine)
    first, second = columns[:, boards : boards + 1], columns[:, boards + 1 : boards + 2]
    aparts = []
    for h in range(hands):
        there = cards[:, h * width : (h + 1) * width].astype(jnp.float32)
        one, two = there[0:1], there[1:2]
        shared = (first == one) | (first == two) | (second == one) | (second == two)
        aparts.append(jnp.where(shared, 0.0, 1.0))
    apart = jnp.concatenate(aparts, axis=1)
    tall = -(-each // 8) * 8
    wide[...] = payload[...].astype(jnp.int32).astype(jnp.float32)
    unit = row_tops(pot, turn_act, flop_act, (each - 2) // 2) * (1.0 / 65535.0)
    sums, turn_cards = [], []
    for b in range(boards):
        x = jnp.concatenate(
            [wide[h, half, pl.ds(b, each, stride=boards), :] for h in range(hands) for half in range(halves)],
            axis=1,
        )
        theirs = x[each - 2 : each - 1]
        turn_cards.append(x[each - 1 : each, :128])
        x = jnp.concatenate([x, jnp.zeros((tall - each, hands * width), jnp.float32)], axis=0)
        x += 32768.0
        high = jnp.floor(x * (1.0 / 256.0))
        pieces = jnp.concatenate([high, x - high * 256.0], axis=0).astype(jnp.bfloat16)
        sign = jnp.clip(columns[:, b : b + 1] - theirs, -1.0, 1.0)
        tile = (sign * apart).astype(jnp.bfloat16)
        part = lax.dot_general(
            pieces, tile, (((1,), (1,)), ((), ())), preferred_element_type=jnp.float32
        )
        part = (part[:tall] * 256.0 + part[tall:]) * unit
        sums.append(part * live[b : b + 1, :].astype(jnp.float32))
    return sums, turn_cards, (each - 2) // 2


def showdown_all(payload, ranks, live, cards, pot, turn_act, flop_act, out, dense, wide):
    sums, turn_cards, actions = board_values(
        payload, ranks, live, cards, pot, turn_act, flop_act, wide
    )
    width = sums[0].shape[1]
    flops = sums[0]
    for part in sums[1:]:
        flops += part
    slot = lax.broadcasted_iota(jnp.int32, (SLOTS, 128), 0)
    hits = [(slot.astype(jnp.float32) == card).astype(jnp.float32) for card in turn_cards]
    flop = (slot == TURNS).astype(jnp.float32)
    for a in range(actions):
        for half in range(width // 128):
            lanes = slice(half * 128, half * 128 + 128)
            block = flop * flops[actions + a : actions + a + 1, lanes]
            for hit, part in zip(hits, sums):
                block += hit * part[a : a + 1, lanes]
            column = a * (width // 128) + half
            for tile in range(SLOTS // 8):
                dense[pl.ds(place(column, tile), 8), :] = block[tile * 8 : tile * 8 + 8]
    spots = {place(c, t) for c in range(actions * (width // 128)) for t in range(SLOTS // 8)}
    for spot in sorted(set(range(0, UNITS * 8, 8)) - spots):
        dense[pl.ds(spot, 8), :] = jnp.zeros((8, 128), jnp.float32)
    for k in range(PLANE):
        out[k] = pack(dense[pl.ds(k * CHUNK, CHUNK), :])


def showdown(payload, ranks, live, cards, pot, turn_act, flop_act, out, rows, wide):
    sums, turn_cards, actions = board_values(
        payload, ranks, live, cards, pot, turn_act, flop_act, wide
    )
    halves = sums[0].shape[1] // 128
    flops = sums[0]
    for part in sums[1:]:
        flops += part
    rows[...] = jnp.zeros_like(rows)
    for b, part in enumerate(sums):
        for half in range(halves):
            lanes = slice(half * 128, half * 128 + 128)
            rows[pl.ds((b * halves + half) * actions, actions), :] = part[:actions, lanes]
    for half in range(halves):
        lanes = slice(half * 128, half * 128 + 128)
        at = (len(sums) * halves + half) * actions
        rows[pl.ds(at, actions), :] = flops[actions : 2 * actions, lanes]
    x = rows[...]
    row = lax.broadcasted_iota(jnp.int32, x.shape, 0)
    lane = lax.broadcasted_iota(jnp.int32, x.shape, 1)
    codes, log = encode(x)
    logs = jnp.sum(jnp.where(row == lane, log, 0.0), axis=0, keepdims=True)
    ids = jnp.zeros((1, 128), jnp.float32)
    for b, card in enumerate(turn_cards):
        ids = jnp.where(lane[:1] == b, card, ids)
    codes = jnp.where(row == BOARD_SCALES, logs, codes)
    codes = jnp.where(row == BOARD_SCALES + 1, ids, codes)
    codes = codes.astype(jnp.int32).astype(jnp.int16)
    for k in range(out.shape[0]):
        out[k] = codes


def run_sums(blocks, out, rows, page):
    count = blocks.shape[0]
    boards, halves, actions = 4, 2, 9
    tails = [blocks[k, 80:96, :].astype(jnp.int32).astype(jnp.float32) for k in range(count)]
    at = BOARD_SCALES - 80
    logs = jnp.concatenate([tail[at : at + 1] for tail in tails], axis=0)
    scales = jnp.transpose(jnp.exp2(logs * (1.0 / 256.0)) * (1.0 / STEPS))
    for k in range(count):
        codes = blocks[k].astype(jnp.int32).astype(jnp.float32)
        rows[k] = codes * scales[:96, k : k + 1]
    ids = [tail[at + 1 : at + 2] for tail in tails]
    least = ids[0][:, 0:1]
    most = ids[-1][:, boards - 1 : boards]
    slot = lax.broadcasted_iota(jnp.int32, (PAGE, 128), 0).astype(jnp.float32)
    hits = [
        [(slot == ids[k][:, b : b + 1] - least).astype(jnp.float32) for b in range(boards)]
        for k in range(count)
    ]
    page[...] = jnp.zeros_like(page)
    for a in range(actions):
        for half in range(halves):
            block = jnp.zeros((PAGE, 128), jnp.float32)
            for k in range(count):
                for b in range(boards):
                    block += hits[k][b] * rows[k, pl.ds((b * halves + half) * actions + a, 1), :]
            page[pl.ds((a * halves + half) * PAGE, PAGE), :] = block
    top, flops = boards * halves * actions, halves * actions
    total = rows[0, pl.ds(top, flops), :]
    for k in range(1, count):
        total += rows[k, pl.ds(top, flops), :]
    page[pl.ds(FLOPS, flops), :] = total
    x = page[...]
    row = lax.broadcasted_iota(jnp.int32, x.shape, 0)
    lane = lax.broadcasted_iota(jnp.int32, x.shape, 1)
    codes, log = encode(x)
    for part in range(2):
        logs = jnp.sum(jnp.where(row == lane + 128 * part, log, 0.0), axis=0, keepdims=True)
        codes = jnp.where(row == PAGE_SCALES + part, logs, codes)
    codes = jnp.where(row == PAGE_SCALES + 2, least, codes)
    codes = jnp.where(row == PAGE_SCALES + 3, most - least + 1.0, codes)
    codes = codes.astype(jnp.int32).astype(jnp.int16)
    for k in range(out.shape[0]):
        out[k] = codes


def finish(turns_over_boards, over_boards, blocks, turn_regret, flop_regret, turn_out, flop_out, values, cards, dense):
    actions, turns, width = turn_regret.shape
    halves, count = width // 128, blocks.shape[0]
    at = PAGE_SCALES - 160
    tails = [blocks[k, 160:176, :].astype(jnp.int32).astype(jnp.float32) for k in range(count)]
    scales = [
        jnp.transpose(
            jnp.exp2(jnp.concatenate([tail[at + part : at + part + 1] for tail in tails], axis=0) * (1.0 / 256.0))
            * (1.0 / STEPS)
        )
        for part in range(2)
    ]
    held = jnp.concatenate([tail[at + 3 : at + 4] for tail in tails], axis=0)
    cards[0] = jnp.max(held).astype(jnp.int32)
    leasts = [jnp.max(tail[at + 2 : at + 3]).astype(jnp.int32) for tail in tails]
    dense[...] = jnp.zeros_like(dense)
    flops = jnp.zeros((32, 128), jnp.float32)
    for k in range(count):
        codes = blocks[k].astype(jnp.int32).astype(jnp.float32)
        early = codes[:128] * scales[0][:, k : k + 1]
        late = codes[128:] * scales[1][:48, k : k + 1]
        flops += late[16:48]
        least = leasts[k]
        for column in range(actions * halves):
            start = column * PAGE
            tile = early[start : start + PAGE] if start < 128 else late[start - 128 : start - 128 + PAGE]
            dense[pl.ds(column * SPAN + least, PAGE), :] += tile
    for half in range(halves):
        lanes = pl.ds(half * 128, 128)
        weighted = jnp.zeros((turns, 128), jnp.float32)
        weight = jnp.zeros((turns, 128), jnp.float32)
        for a in range(actions):
            q = dense[pl.ds((a * halves + half) * SPAN, turns), :] * turns_over_boards
            regret = turn_regret[a, :, lanes]
            weighted += regret * q
            weight += regret
        value = weighted / weight
        values[:, lanes] = value
        early = flop_regret[:, lanes]
        flop_q = flops[half * actions : half * actions + actions] * over_boards
        root = jnp.sum(early * flop_q, axis=0, keepdims=True) / jnp.sum(early, axis=0, keepdims=True)
        flop_out[:, lanes] = jnp.maximum(early + flop_q - root, 0.0)
        for a in range(actions):
            q = dense[pl.ds((a * halves + half) * SPAN, turns), :] * turns_over_boards
            turn_out[a, :, lanes] = jnp.maximum(turn_regret[a, :, lanes] + q - value, 0.0)


def add_up(blocks, out):
    total = jnp.zeros((CHUNK, 128), jnp.float32)
    for block in unpack(blocks):
        total += block
    row = lax.broadcasted_iota(jnp.int32, total.shape, 0)
    codes = pack(jnp.where(row == SCALES, 0.0, total))
    for k in range(out.shape[0]):
        out[k] = codes


def settle(turns_over_boards, over_boards, blocks, turn_regret, flop_regret, turn_out, flop_out, values, sums):
    actions, turns, width = turn_regret.shape
    halves = width // 128
    for k, block in enumerate(unpack(blocks)):
        sums[pl.ds(k * CHUNK, CHUNK), :] = block

    def column(at):
        tiles = [sums[pl.ds(place(at, tile), 8), :] for tile in range(SLOTS // 8)]
        whole = jnp.concatenate(tiles, axis=0)
        return whole[:turns] * turns_over_boards, whole[turns : turns + 1] * over_boards

    for half in range(halves):
        lanes = pl.ds(half * 128, 128)
        weighted = jnp.zeros((turns, 128), jnp.float32)
        weight = jnp.zeros((turns, 128), jnp.float32)
        top = jnp.zeros((1, 128), jnp.float32)
        bottom = jnp.zeros((1, 128), jnp.float32)
        for a in range(actions):
            q, flop_q = column(a * halves + half)
            regret = turn_regret[a, :, lanes]
            weighted += regret * q
            weight += regret
            early = flop_regret[a : a + 1, lanes]
            top += early * flop_q
            bottom += early
        value = weighted / weight
        values[:, lanes] = value
        root = top / bottom
        for a in range(actions):
            q, flop_q = column(a * halves + half)
            turn_out[a, :, lanes] = jnp.maximum(turn_regret[a, :, lanes] + q - value, 0.0)
            early = flop_regret[a : a + 1, lanes]
            flop_out[a : a + 1, lanes] = jnp.maximum(early + flop_q - root, 0.0)


def shards(
    reach, ranks, live, turn_of, hand_cards, pot, turn_act, flop_act, turn_regret, flop_regret
):
    boards, seqs, width = reach.shape
    total_hands = hand_cards.shape[1]
    turns, actions, _ = turn_regret.shape
    rows = 2 * actions * boards
    boards_all = boards * lax.axis_size("turn")
    params = pltpu.CompilerParams(vmem_limit_bytes=VMEM)
    f32 = jnp.float32

    acts = tuple(x.reshape(1, seqs) for x in (pot, turn_act, flop_act))
    operands = (pot, turn_act, flop_act, turn_of, jnp.transpose(reach, (1, 0, 2)), ranks, live) + acts
    payload = pl.pallas_call(
        weigh,
        out_shape=jax.ShapeDtypeStruct((width // 128, rows + 2 * boards, 128), jnp.int16),
        in_specs=[pl.BlockSpec(memory_space=pltpu.HBM)] * 10,
        out_specs=pl.BlockSpec(memory_space=pltpu.VMEM),
        scratch_shapes=[
            pltpu.SMEM(pot.shape, f32),
            pltpu.SMEM(turn_act.shape, jnp.int32),
            pltpu.SMEM(flop_act.shape, jnp.int32),
            pltpu.SMEM(turn_of.shape, jnp.int32),
            pltpu.VMEM((seqs, boards, width), reach.dtype),
            pltpu.VMEM(ranks.shape, jnp.int32),
            pltpu.VMEM(live.shape, jnp.int32),
            *[pltpu.VMEM((1, seqs), x.dtype) for x in acts],
            pltpu.VMEM((width // 128, rows + 2 * boards, 128), f32),
            pltpu.SemaphoreType.DMA((10,)),
            *[pltpu.VMEM((actions, boards, width), f32)] * (2 * BANKS),
        ],
        compiler_params=params,
    )(*[pltpu.with_memory_space_constraint(x, pltpu.HBM) for x in operands])

    gathered = lax.all_gather(payload, "hand", axis=0, tiled=False)

    planes = [[k * LINE + z for k in range(PLANE)] for z in range(LINE)]
    lines = [[k * LINE + z for z in range(LINE)] for k in range(PLANE)]
    vmem = pl.BlockSpec(memory_space=pltpu.VMEM)
    factors = (turns / boards_all / total_hands, 1.0 / boards_all / total_hands)
    by_action = jnp.transpose(turn_regret, (1, 0, 2))
    outputs = (
        jax.ShapeDtypeStruct((actions, turns, width), f32),
        jax.ShapeDtypeStruct((actions, width), f32),
        jax.ShapeDtypeStruct((turns, width), f32),
    )

    def call(kernel, shape, scratch, *args):
        return pl.pallas_call(
            kernel,
            out_shape=jax.ShapeDtypeStruct(shape, jnp.int16),
            in_specs=spread(len(args)),
            out_specs=vmem,
            scratch_shapes=[pltpu.VMEM(dims, f32) for dims in scratch],
            compiler_params=params,
        )(*args)

    def swap(blocks, groups):
        return lax.all_to_all(blocks, "turn", 0, 0, axis_index_groups=groups, tiled=True)

    blocks = call(
        showdown, (LINE, BOARD_ROWS, 128), [(BOARD_ROWS, 128), gathered.shape],
        gathered, ranks, live, hand_cards, *acts
    )
    blocks = swap(blocks, lines)
    blocks = call(
        run_sums, (PLANE, PAGE_ROWS, 128), [(LINE, BOARD_ROWS, 128), (PAGE_ROWS, 128)], blocks
    )
    blocks = swap(blocks, planes)
    turn_out, flop_out, values, cards = pl.pallas_call(
        lambda *refs: finish(*factors, *refs),
        out_shape=outputs + (jax.ShapeDtypeStruct((1,), jnp.int32),),
        in_specs=spread(3),
        out_specs=tuple(spread(3)) + (pl.BlockSpec(memory_space=pltpu.SMEM),),
        scratch_shapes=[pltpu.VMEM((actions * (width // 128) * SPAN, 128), f32)],
        compiler_params=params,
    )(blocks, by_action, flop_regret)

    def every_card(state):
        payload = gathered + jnp.where(state[0] > PAGE, 0, 1).astype(jnp.int16)
        scratch = [(UNITS * 8, 128), gathered.shape]
        chunks = call(
            showdown_all, (PLANE, CHUNK, 128), scratch, payload, ranks, live, hand_cards, *acts
        )
        chunks = swap(chunks, planes)
        chunks = swap(call(add_up, (LINE, CHUNK, 128), [], chunks), lines)
        chunks = swap(call(add_up, (PLANE, CHUNK, 128), [], chunks), planes)
        results = pl.pallas_call(
            lambda *refs: settle(*factors, *refs),
            out_shape=outputs,
            in_specs=spread(3),
            out_specs=tuple(spread(3)),
            scratch_shapes=[pltpu.VMEM((UNITS * 8, 128), f32)],
            compiler_params=params,
        )(chunks, by_action, flop_regret)
        return (jnp.int32(0),) + tuple(results)

    state = (cards[0], turn_out, flop_out, values)
    _, turn_out, flop_out, values = lax.while_loop(lambda s: s[0] > PAGE, every_card, state)
    return (jnp.transpose(turn_out, (1, 0, 2)), flop_out, values)


def solution(mesh):
    return jax.shard_map(
        shards,
        mesh=mesh,
        in_specs=(
            P("turn", None, "hand"),
            P("turn", "hand"),
            P("turn", "hand"),
            P("turn"),
            P(),
            P(),
            P(),
            P(),
            P(None, None, "hand"),
            P(None, "hand"),
        ),
        out_specs=(P(None, None, "hand"), P(None, "hand"), P(None, "hand")),
        check_vma=False,
    )
```

```python
import jax
import jax.numpy as jnp
from jax import lax
from jax.experimental import pallas as pl
from jax.experimental.pallas import tpu as pltpu
from jax.sharding import PartitionSpec as P

TURNS = 49
SLOTS = 56
UNITS = 128
PLANE = 16
LINE = 8
CHUNK = UNITS * 8 // PLANE
STEPS = 32760.0
SCALES = 58
BOARD_ROWS = 96
BOARD_SCALES = 90
PAGE = 8
FLOPS = 144
PAGE_SCALES = 162
PAGE_ROWS = 176
SPAN = 64
VMEM = 48 * 1024 * 1024
BANKS = 4


def spread(count):
    return [pl.BlockSpec(memory_space=pltpu.VMEM)] * count


def place(column, tile):
    columns, tiles = UNITS // (SLOTS // 8), SLOTS // 8
    if tile == tiles - 1 and column < PLANE:
        return column * CHUNK + CHUNK - 8
    spot = column * (tiles - 1) + tile if tile < tiles - 1 else columns * (tiles - 1) + column - PLANE
    return spot // 7 * CHUNK + spot % 7 * 8


def encode(x):
    top = jnp.maximum(jnp.max(jnp.abs(x), axis=1, keepdims=True), 1e-30)
    log = jnp.ceil(jnp.log2(top) * 256.0)
    return jnp.round(x * (STEPS / jnp.exp2(log * (1.0 / 256.0)))), log


def pack(x):
    row = lax.broadcasted_iota(jnp.int32, x.shape, 0)
    lane = lax.broadcasted_iota(jnp.int32, x.shape, 1)
    codes, log = encode(x)
    logs = jnp.sum(jnp.where(row == lane, log, 0.0), axis=0, keepdims=True)
    return jnp.where(row == SCALES, logs, codes).astype(jnp.int32).astype(jnp.int16)


def unpack(blocks):
    count = blocks.shape[0]
    ends = [blocks[k, 48:64, :].astype(jnp.int32).astype(jnp.float32) for k in range(count)]
    logs = jnp.concatenate([end[SCALES - 48 : SCALES - 47] for end in ends], axis=0)
    scales = jnp.transpose(jnp.exp2(logs * (1.0 / 256.0)) * (1.0 / STEPS))
    for k in range(count):
        codes = blocks[k].astype(jnp.int32).astype(jnp.float32)
        yield codes * scales[:64, k : k + 1]


def row_tops(pot, turn_act, flop_act, count):
    row = lax.broadcasted_iota(jnp.int32, (24, pot.shape[1]), 0)
    key = jnp.where(row < count, turn_act[...], flop_act[...] + count)
    return jnp.sum(jnp.where(row == key, pot[...], 0.0), axis=1, keepdims=True)


def weigh(
    pot_hbm, turn_hbm, flop_hbm, of_hbm, reach_hbm, ranks_hbm, live_hbm, pots_hbm, turns_hbm, flops_hbm, out, tops,
    pot, turn_act, flop_act, turn_of, reach, ranks, live, pots, turns, flops, stage, sems, *banks
):
    pairs = (
        (reach_hbm, reach), (pot_hbm, pot), (turn_hbm, turn_act), (flop_hbm, flop_act),
        (of_hbm, turn_of), (ranks_hbm, ranks), (live_hbm, live),
        (pots_hbm, pots), (turns_hbm, turns), (flops_hbm, flops),
    )
    moves = [pltpu.make_async_copy(x, y, sems.at[k]) for k, (x, y) in enumerate(pairs)]
    for move in moves:
        move.start()
    turn_sums, flop_sums = banks[:BANKS], banks[BANKS:]
    for bank in banks:
        bank[...] = jnp.zeros_like(bank)
    for move in moves:
        move.wait()
    seqs, boards, width = reach.shape
    halves = [slice(half * 128, half * 128 + 128) for half in range(width // 128)]
    for s in range(seqs):
        term = reach[s].astype(jnp.float32) * pot[s]
        turn_sums[s % BANKS][turn_act[s]] += term
        flop_sums[s % BANKS][flop_act[s]] += term
    alive = live[...].astype(jnp.float32)
    most = row_tops(pots, turns, flops, turn_sums[0].shape[0])
    tops[...] = jnp.broadcast_to(most, tops.shape)
    steps = 65535.0 / jnp.maximum(most, 1e-30)
    top = 0
    for sums in (turn_sums, flop_sums):
        for r in range(sums[0].shape[0]):
            total = sums[0][r]
            for other in sums[1:]:
                total += other[r]
            at = top // boards
            total = jnp.round(total * alive * steps[at : at + 1])
            total = jnp.minimum(total, 65535.0) - 32768.0
            for half, lanes in enumerate(halves):
                stage[half, pl.ds(top, boards), :] = total[:, lanes]
            top += boards
    for half, lanes in enumerate(halves):
        stage[half, pl.ds(top, boards), :] = ranks[:, lanes].astype(jnp.float32)
        for b in range(boards):
            card = jnp.full((1, 128), turn_of[b], jnp.int32).astype(jnp.float32)
            stage[half, pl.ds(top + boards + b, 1), :] = card
    out[...] = stage[...].astype(jnp.int32).astype(jnp.int16)


def board_values(payload, tops, ranks, live, cards, wide):
    hands, halves, rows, _ = payload.shape
    width = halves * 128
    boards = ranks.shape[0]
    each = rows // boards
    me = lax.axis_index("hand")
    here = cards[:, pl.ds(pl.multiple_of(me * width, width), width)].astype(jnp.float32)
    mine = jnp.concatenate(
        [ranks[...].astype(jnp.float32), here, jnp.zeros((2, width), jnp.float32)], axis=0
    )
    columns = jnp.transpose(mine)
    first, second = columns[:, boards : boards + 1], columns[:, boards + 1 : boards + 2]
    aparts = []
    for h in range(hands):
        there = cards[:, h * width : (h + 1) * width].astype(jnp.float32)
        one, two = there[0:1], there[1:2]
        shared = (first == one) | (first == two) | (second == one) | (second == two)
        aparts.append(jnp.where(shared, 0.0, 1.0))
    apart = jnp.concatenate(aparts, axis=1)
    tall = -(-each // 8) * 8
    wide[...] = payload[...].astype(jnp.int32).astype(jnp.float32)
    unit = tops[:, 0:1] * (1.0 / 65535.0)
    sums, turn_cards = [], []
    for b in range(boards):
        x = jnp.concatenate(
            [wide[h, half, pl.ds(b, each, stride=boards), :] for h in range(hands) for half in range(halves)],
            axis=1,
        )
        theirs = x[each - 2 : each - 1]
        turn_cards.append(x[each - 1 : each, :128])
        x = jnp.concatenate([x, jnp.zeros((tall - each, hands * width), jnp.float32)], axis=0)
        x += 32768.0
        high = jnp.floor(x * (1.0 / 256.0))
        pieces = jnp.concatenate([high, x - high * 256.0], axis=0).astype(jnp.bfloat16)
        sign = jnp.clip(columns[:, b : b + 1] - theirs, -1.0, 1.0)
        tile = (sign * apart).astype(jnp.bfloat16)
        part = lax.dot_general(
            pieces, tile, (((1,), (1,)), ((), ())), preferred_element_type=jnp.float32
        )
        part = (part[:tall] * 256.0 + part[tall:]) * unit
        sums.append(part * live[b : b + 1, :].astype(jnp.float32))
    return sums, turn_cards, (each - 2) // 2


def showdown_all(payload, tops, ranks, live, cards, out, dense, wide):
    sums, turn_cards, actions = board_values(payload, tops, ranks, live, cards, wide)
    width = sums[0].shape[1]
    flops = sums[0]
    for part in sums[1:]:
        flops += part
    slot = lax.broadcasted_iota(jnp.int32, (SLOTS, 128), 0)
    hits = [(slot.astype(jnp.float32) == card).astype(jnp.float32) for card in turn_cards]
    flop = (slot == TURNS).astype(jnp.float32)
    for a in range(actions):
        for half in range(width // 128):
            lanes = slice(half * 128, half * 128 + 128)
            block = flop * flops[actions + a : actions + a + 1, lanes]
            for hit, part in zip(hits, sums):
                block += hit * part[a : a + 1, lanes]
            column = a * (width // 128) + half
            for tile in range(SLOTS // 8):
                dense[pl.ds(place(column, tile), 8), :] = block[tile * 8 : tile * 8 + 8]
    spots = {place(c, t) for c in range(actions * (width // 128)) for t in range(SLOTS // 8)}
    for spot in sorted(set(range(0, UNITS * 8, 8)) - spots):
        dense[pl.ds(spot, 8), :] = jnp.zeros((8, 128), jnp.float32)
    for k in range(PLANE):
        out[k] = pack(dense[pl.ds(k * CHUNK, CHUNK), :])


def showdown(payload, tops, ranks, live, cards, out, rows, wide):
    sums, turn_cards, actions = board_values(payload, tops, ranks, live, cards, wide)
    halves = sums[0].shape[1] // 128
    flops = sums[0]
    for part in sums[1:]:
        flops += part
    rows[...] = jnp.zeros_like(rows)
    for b, part in enumerate(sums):
        for half in range(halves):
            lanes = slice(half * 128, half * 128 + 128)
            rows[pl.ds((b * halves + half) * actions, actions), :] = part[:actions, lanes]
    for half in range(halves):
        lanes = slice(half * 128, half * 128 + 128)
        at = (len(sums) * halves + half) * actions
        rows[pl.ds(at, actions), :] = flops[actions : 2 * actions, lanes]
    x = rows[...]
    row = lax.broadcasted_iota(jnp.int32, x.shape, 0)
    lane = lax.broadcasted_iota(jnp.int32, x.shape, 1)
    codes, log = encode(x)
    logs = jnp.sum(jnp.where(row == lane, log, 0.0), axis=0, keepdims=True)
    ids = jnp.zeros((1, 128), jnp.float32)
    for b, card in enumerate(turn_cards):
        ids = jnp.where(lane[:1] == b, card, ids)
    codes = jnp.where(row == BOARD_SCALES, logs, codes)
    codes = jnp.where(row == BOARD_SCALES + 1, ids, codes)
    codes = codes.astype(jnp.int32).astype(jnp.int16)
    for k in range(out.shape[0]):
        out[k] = codes


def run_sums(blocks, out, rows, page):
    count = blocks.shape[0]
    boards, halves, actions = 4, 2, 9
    tails = [blocks[k, 80:96, :].astype(jnp.int32).astype(jnp.float32) for k in range(count)]
    at = BOARD_SCALES - 80
    logs = jnp.concatenate([tail[at : at + 1] for tail in tails], axis=0)
    scales = jnp.transpose(jnp.exp2(logs * (1.0 / 256.0)) * (1.0 / STEPS))
    for k in range(count):
        codes = blocks[k].astype(jnp.int32).astype(jnp.float32)
        rows[k] = codes * scales[:96, k : k + 1]
    ids = [tail[at + 1 : at + 2] for tail in tails]
    least = ids[0][:, 0:1]
    most = ids[-1][:, boards - 1 : boards]
    slot = lax.broadcasted_iota(jnp.int32, (PAGE, 128), 0).astype(jnp.float32)
    hits = [
        [(slot == ids[k][:, b : b + 1] - least).astype(jnp.float32) for b in range(boards)]
        for k in range(count)
    ]
    page[...] = jnp.zeros_like(page)
    for a in range(actions):
        for half in range(halves):
            block = jnp.zeros((PAGE, 128), jnp.float32)
            for k in range(count):
                for b in range(boards):
                    block += hits[k][b] * rows[k, pl.ds((b * halves + half) * actions + a, 1), :]
            page[pl.ds((a * halves + half) * PAGE, PAGE), :] = block
    top, flops = boards * halves * actions, halves * actions
    total = rows[0, pl.ds(top, flops), :]
    for k in range(1, count):
        total += rows[k, pl.ds(top, flops), :]
    page[pl.ds(FLOPS, flops), :] = total
    x = page[...]
    row = lax.broadcasted_iota(jnp.int32, x.shape, 0)
    lane = lax.broadcasted_iota(jnp.int32, x.shape, 1)
    codes, log = encode(x)
    for part in range(2):
        logs = jnp.sum(jnp.where(row == lane + 128 * part, log, 0.0), axis=0, keepdims=True)
        codes = jnp.where(row == PAGE_SCALES + part, logs, codes)
    codes = jnp.where(row == PAGE_SCALES + 2, least, codes)
    codes = jnp.where(row == PAGE_SCALES + 3, most - least + 1.0, codes)
    codes = codes.astype(jnp.int32).astype(jnp.int16)
    for k in range(out.shape[0]):
        out[k] = codes


def finish(turns_over_boards, over_boards, blocks, turn_regret, flop_regret, turn_out, flop_out, values, cards, dense):
    actions, turns, width = turn_regret.shape
    halves, count = width // 128, blocks.shape[0]
    at = PAGE_SCALES - 160
    tails = [blocks[k, 160:176, :].astype(jnp.int32).astype(jnp.float32) for k in range(count)]
    scales = [
        jnp.transpose(
            jnp.exp2(jnp.concatenate([tail[at + part : at + part + 1] for tail in tails], axis=0) * (1.0 / 256.0))
            * (1.0 / STEPS)
        )
        for part in range(2)
    ]
    held = jnp.concatenate([tail[at + 3 : at + 4] for tail in tails], axis=0)
    cards[0] = jnp.max(held).astype(jnp.int32)
    leasts = [jnp.max(tail[at + 2 : at + 3]).astype(jnp.int32) for tail in tails]
    dense[...] = jnp.zeros_like(dense)
    flops = jnp.zeros((32, 128), jnp.float32)
    for k in range(count):
        codes = blocks[k].astype(jnp.int32).astype(jnp.float32)
        early = codes[:128] * scales[0][:, k : k + 1]
        late = codes[128:] * scales[1][:48, k : k + 1]
        flops += late[16:48]
        least = leasts[k]
        for column in range(actions * halves):
            start = column * PAGE
            tile = early[start : start + PAGE] if start < 128 else late[start - 128 : start - 128 + PAGE]
            dense[pl.ds(column * SPAN + least, PAGE), :] += tile
    for half in range(halves):
        lanes = pl.ds(half * 128, 128)
        weighted = jnp.zeros((turns, 128), jnp.float32)
        weight = jnp.zeros((turns, 128), jnp.float32)
        for a in range(actions):
            q = dense[pl.ds((a * halves + half) * SPAN, turns), :] * turns_over_boards
            regret = turn_regret[a, :, lanes]
            weighted += regret * q
            weight += regret
        value = weighted / weight
        values[:, lanes] = value
        early = flop_regret[:, lanes]
        flop_q = flops[half * actions : half * actions + actions] * over_boards
        root = jnp.sum(early * flop_q, axis=0, keepdims=True) / jnp.sum(early, axis=0, keepdims=True)
        flop_out[:, lanes] = jnp.maximum(early + flop_q - root, 0.0)
        for a in range(actions):
            q = dense[pl.ds((a * halves + half) * SPAN, turns), :] * turns_over_boards
            turn_out[a, :, lanes] = jnp.maximum(turn_regret[a, :, lanes] + q - value, 0.0)


def add_up(blocks, out):
    total = jnp.zeros((CHUNK, 128), jnp.float32)
    for block in unpack(blocks):
        total += block
    row = lax.broadcasted_iota(jnp.int32, total.shape, 0)
    codes = pack(jnp.where(row == SCALES, 0.0, total))
    for k in range(out.shape[0]):
        out[k] = codes


def settle(turns_over_boards, over_boards, blocks, turn_regret, flop_regret, turn_out, flop_out, values, sums):
    actions, turns, width = turn_regret.shape
    halves = width // 128
    for k, block in enumerate(unpack(blocks)):
        sums[pl.ds(k * CHUNK, CHUNK), :] = block

    def column(at):
        tiles = [sums[pl.ds(place(at, tile), 8), :] for tile in range(SLOTS // 8)]
        whole = jnp.concatenate(tiles, axis=0)
        return whole[:turns] * turns_over_boards, whole[turns : turns + 1] * over_boards

    for half in range(halves):
        lanes = pl.ds(half * 128, 128)
        weighted = jnp.zeros((turns, 128), jnp.float32)
        weight = jnp.zeros((turns, 128), jnp.float32)
        top = jnp.zeros((1, 128), jnp.float32)
        bottom = jnp.zeros((1, 128), jnp.float32)
        for a in range(actions):
            q, flop_q = column(a * halves + half)
            regret = turn_regret[a, :, lanes]
            weighted += regret * q
            weight += regret
            early = flop_regret[a : a + 1, lanes]
            top += early * flop_q
            bottom += early
        value = weighted / weight
        values[:, lanes] = value
        root = top / bottom
        for a in range(actions):
            q, flop_q = column(a * halves + half)
            turn_out[a, :, lanes] = jnp.maximum(turn_regret[a, :, lanes] + q - value, 0.0)
            early = flop_regret[a : a + 1, lanes]
            flop_out[a : a + 1, lanes] = jnp.maximum(early + flop_q - root, 0.0)


def shards(
    reach, ranks, live, turn_of, hand_cards, pot, turn_act, flop_act, turn_regret, flop_regret
):
    boards, seqs, width = reach.shape
    total_hands = hand_cards.shape[1]
    turns, actions, _ = turn_regret.shape
    rows = 2 * actions * boards
    boards_all = boards * lax.axis_size("turn")
    params = pltpu.CompilerParams(vmem_limit_bytes=VMEM)
    f32 = jnp.float32

    acts = tuple(x.reshape(1, seqs) for x in (pot, turn_act, flop_act))
    operands = (pot, turn_act, flop_act, turn_of, jnp.transpose(reach, (1, 0, 2)), ranks, live) + acts
    payload, tops = pl.pallas_call(
        weigh,
        out_shape=(
            jax.ShapeDtypeStruct((width // 128, rows + 2 * boards, 128), jnp.int16),
            jax.ShapeDtypeStruct((24, 128), f32),
        ),
        in_specs=[pl.BlockSpec(memory_space=pltpu.HBM)] * 10,
        out_specs=tuple(spread(2)),
        scratch_shapes=[
            pltpu.SMEM(pot.shape, f32),
            pltpu.SMEM(turn_act.shape, jnp.int32),
            pltpu.SMEM(flop_act.shape, jnp.int32),
            pltpu.SMEM(turn_of.shape, jnp.int32),
            pltpu.VMEM((seqs, boards, width), reach.dtype),
            pltpu.VMEM(ranks.shape, jnp.int32),
            pltpu.VMEM(live.shape, jnp.int32),
            *[pltpu.VMEM((1, seqs), x.dtype) for x in acts],
            pltpu.VMEM((width // 128, rows + 2 * boards, 128), f32),
            pltpu.SemaphoreType.DMA((10,)),
            *[pltpu.VMEM((actions, boards, width), f32)] * (2 * BANKS),
        ],
        compiler_params=params,
    )(*[pltpu.with_memory_space_constraint(x, pltpu.HBM) for x in operands])

    gathered = lax.all_gather(payload, "hand", axis=0, tiled=False)

    planes = [[k * LINE + z for k in range(PLANE)] for z in range(LINE)]
    lines = [[k * LINE + z for z in range(LINE)] for k in range(PLANE)]
    vmem = pl.BlockSpec(memory_space=pltpu.VMEM)
    factors = (turns / boards_all / total_hands, 1.0 / boards_all / total_hands)
    by_action = jnp.transpose(turn_regret, (1, 0, 2))
    outputs = (
        jax.ShapeDtypeStruct((actions, turns, width), f32),
        jax.ShapeDtypeStruct((actions, width), f32),
        jax.ShapeDtypeStruct((turns, width), f32),
    )

    def call(kernel, shape, scratch, *args):
        return pl.pallas_call(
            kernel,
            out_shape=jax.ShapeDtypeStruct(shape, jnp.int16),
            in_specs=spread(len(args)),
            out_specs=vmem,
            scratch_shapes=[pltpu.VMEM(dims, f32) for dims in scratch],
            compiler_params=params,
        )(*args)

    def swap(blocks, groups):
        return lax.all_to_all(blocks, "turn", 0, 0, axis_index_groups=groups, tiled=True)

    blocks = call(
        showdown, (LINE, BOARD_ROWS, 128), [(BOARD_ROWS, 128), gathered.shape],
        gathered, tops, ranks, live, hand_cards
    )
    blocks = swap(blocks, lines)
    blocks = call(
        run_sums, (PLANE, PAGE_ROWS, 128), [(LINE, BOARD_ROWS, 128), (PAGE_ROWS, 128)], blocks
    )
    blocks = swap(blocks, planes)
    turn_out, flop_out, values, cards = pl.pallas_call(
        lambda *refs: finish(*factors, *refs),
        out_shape=outputs + (jax.ShapeDtypeStruct((1,), jnp.int32),),
        in_specs=spread(3),
        out_specs=tuple(spread(3)) + (pl.BlockSpec(memory_space=pltpu.SMEM),),
        scratch_shapes=[pltpu.VMEM((actions * (width // 128) * SPAN, 128), f32)],
        compiler_params=params,
    )(blocks, by_action, flop_regret)

    def every_card(state):
        payload = gathered + jnp.where(state[0] > PAGE, 0, 1).astype(jnp.int16)
        scratch = [(UNITS * 8, 128), gathered.shape]
        chunks = call(
            showdown_all, (PLANE, CHUNK, 128), scratch, payload, tops, ranks, live, hand_cards
        )
        chunks = swap(chunks, planes)
        chunks = swap(call(add_up, (LINE, CHUNK, 128), [], chunks), lines)
        chunks = swap(call(add_up, (PLANE, CHUNK, 128), [], chunks), planes)
        results = pl.pallas_call(
            lambda *refs: settle(*factors, *refs),
            out_shape=outputs,
            in_specs=spread(3),
            out_specs=tuple(spread(3)),
            scratch_shapes=[pltpu.VMEM((UNITS * 8, 128), f32)],
            compiler_params=params,
        )(chunks, by_action, flop_regret)
        return (jnp.int32(0),) + tuple(results)

    state = (cards[0], turn_out, flop_out, values)
    _, turn_out, flop_out, values = lax.while_loop(lambda s: s[0] > PAGE, every_card, state)
    return (jnp.transpose(turn_out, (1, 0, 2)), flop_out, values)


def solution(mesh):
    return jax.shard_map(
        shards,
        mesh=mesh,
        in_specs=(
            P("turn", None, "hand"),
            P("turn", "hand"),
            P("turn", "hand"),
            P("turn"),
            P(),
            P(),
            P(),
            P(),
            P(None, None, "hand"),
            P(None, "hand"),
        ),
        out_specs=(P(None, None, "hand"), P(None, "hand"), P(None, "hand")),
        check_vma=False,
    )
```

```python
import jax
import jax.numpy as jnp
from jax import lax
from jax.experimental import pallas as pl
from jax.experimental.pallas import tpu as pltpu
from jax.sharding import PartitionSpec as P

TURNS = 49
SLOTS = 56
UNITS = 128
PLANE = 16
LINE = 8
CHUNK = UNITS * 8 // PLANE
STEPS = 32760.0
SCALES = 58
BOARD_ROWS = 96
BOARD_SCALES = 90
PAGE = 8
FLOPS = 144
PAGE_SCALES = 162
PAGE_ROWS = 176
SPAN = 64
VMEM = 48 * 1024 * 1024
BANKS = 4


def spread(count):
    return [pl.BlockSpec(memory_space=pltpu.VMEM)] * count


def place(column, tile):
    columns, tiles = UNITS // (SLOTS // 8), SLOTS // 8
    if tile == tiles - 1 and column < PLANE:
        return column * CHUNK + CHUNK - 8
    spot = column * (tiles - 1) + tile if tile < tiles - 1 else columns * (tiles - 1) + column - PLANE
    return spot // 7 * CHUNK + spot % 7 * 8


def encode(x):
    top = jnp.maximum(jnp.max(jnp.abs(x), axis=1, keepdims=True), 1e-30)
    log = jnp.ceil(jnp.log2(top) * 256.0)
    return jnp.round(x * (STEPS / jnp.exp2(log * (1.0 / 256.0)))), log


def pack(x):
    row = lax.broadcasted_iota(jnp.int32, x.shape, 0)
    lane = lax.broadcasted_iota(jnp.int32, x.shape, 1)
    codes, log = encode(x)
    logs = jnp.sum(jnp.where(row == lane, log, 0.0), axis=0, keepdims=True)
    return jnp.where(row == SCALES, logs, codes).astype(jnp.int32).astype(jnp.int16)


def unpack(blocks):
    count = blocks.shape[0]
    ends = [blocks[k, 48:64, :].astype(jnp.int32).astype(jnp.float32) for k in range(count)]
    logs = jnp.concatenate([end[SCALES - 48 : SCALES - 47] for end in ends], axis=0)
    scales = jnp.transpose(jnp.exp2(logs * (1.0 / 256.0)) * (1.0 / STEPS))
    for k in range(count):
        codes = blocks[k].astype(jnp.int32).astype(jnp.float32)
        yield codes * scales[:64, k : k + 1]


def row_tops(pot, turn_act, flop_act, count):
    row = lax.broadcasted_iota(jnp.int32, (24, pot.shape[1]), 0)
    key = jnp.where(row < count, turn_act[...], flop_act[...] + count)
    return jnp.sum(jnp.where(row == key, pot[...], 0.0), axis=1, keepdims=True)


def weigh(
    pot_hbm, turn_hbm, flop_hbm, of_hbm, reach_hbm, ranks_hbm, live_hbm, pots_hbm, turns_hbm, flops_hbm, out, tops,
    pot, turn_act, flop_act, turn_of, reach, ranks, live, pots, turns, flops, stage, sems, *banks
):
    pairs = (
        (reach_hbm, reach), (pot_hbm, pot), (turn_hbm, turn_act), (flop_hbm, flop_act),
        (of_hbm, turn_of), (ranks_hbm, ranks), (live_hbm, live),
        (pots_hbm, pots), (turns_hbm, turns), (flops_hbm, flops),
    )
    moves = [pltpu.make_async_copy(x, y, sems.at[k]) for k, (x, y) in enumerate(pairs)]
    for move in moves:
        move.start()
    turn_sums, flop_sums = banks[:BANKS], banks[BANKS:]
    for bank in banks:
        bank[...] = jnp.zeros_like(bank)
    for move in moves:
        move.wait()
    seqs, boards, width = reach.shape
    halves = [slice(half * 128, half * 128 + 128) for half in range(width // 128)]
    for s in range(seqs):
        term = reach[s].astype(jnp.float32) * pot[s]
        turn_sums[s % BANKS][turn_act[s]] += term
        flop_sums[s % BANKS][flop_act[s]] += term
    alive = live[...].astype(jnp.float32)
    most = row_tops(pots, turns, flops, turn_sums[0].shape[0])
    tops[...] = jnp.broadcast_to(most, tops.shape)
    steps = 65535.0 / jnp.maximum(most, 1e-30)
    top = 0
    for sums in (turn_sums, flop_sums):
        for r in range(sums[0].shape[0]):
            total = sums[0][r]
            for other in sums[1:]:
                total += other[r]
            at = top // boards
            total = jnp.round(total * alive * steps[at : at + 1])
            total = jnp.minimum(total, 65535.0) - 32768.0
            for half, lanes in enumerate(halves):
                stage[half, pl.ds(top, boards), :] = total[:, lanes]
            top += boards
    for half, lanes in enumerate(halves):
        stage[half, pl.ds(top, boards), :] = ranks[:, lanes].astype(jnp.float32)
        for b in range(boards):
            card = jnp.full((1, 128), turn_of[b], jnp.int32).astype(jnp.float32)
            stage[half, pl.ds(top + boards + b, 1), :] = card
    out[...] = stage[...].astype(jnp.int32).astype(jnp.int16)


def board_values(payload, tops, ranks, live, cards, wide):
    hands, halves, rows, _ = payload.shape
    width = halves * 128
    boards = ranks.shape[0]
    each = rows // boards
    me = lax.axis_index("hand")
    here = cards[:, pl.ds(pl.multiple_of(me * width, width), width)].astype(jnp.float32)
    mine = jnp.concatenate(
        [ranks[...].astype(jnp.float32), here, jnp.zeros((2, width), jnp.float32)], axis=0
    )
    columns = jnp.transpose(mine)
    first, second = columns[:, boards : boards + 1], columns[:, boards + 1 : boards + 2]
    aparts = []
    for h in range(hands):
        there = cards[:, h * width : (h + 1) * width].astype(jnp.float32)
        one, two = there[0:1], there[1:2]
        shared = (first == one) | (first == two) | (second == one) | (second == two)
        aparts.append(jnp.where(shared, 0.0, 1.0))
    apart = jnp.concatenate(aparts, axis=1)
    tall = -(-each // 8) * 8
    wide[...] = payload[...].astype(jnp.int32).astype(jnp.float32)
    unit = tops[:, 0:1] * (1.0 / 65535.0)
    sums, turn_cards = [], []
    for b in range(boards):
        x = jnp.concatenate(
            [wide[h, half, pl.ds(b, each, stride=boards), :] for h in range(hands) for half in range(halves)],
            axis=1,
        )
        theirs = x[each - 2 : each - 1]
        turn_cards.append(x[each - 1 : each, :128])
        x = jnp.concatenate([x, jnp.zeros((tall - each, hands * width), jnp.float32)], axis=0)
        x += 32768.0
        high = jnp.floor(x * (1.0 / 256.0))
        pieces = jnp.concatenate([high, x - high * 256.0], axis=0).astype(jnp.bfloat16)
        sign = jnp.clip(columns[:, b : b + 1] - theirs, -1.0, 1.0)
        tile = (sign * apart).astype(jnp.bfloat16)
        part = lax.dot_general(
            pieces, tile, (((1,), (1,)), ((), ())), preferred_element_type=jnp.float32
        )
        part = (part[:tall] * 256.0 + part[tall:]) * unit
        sums.append(part * live[b : b + 1, :].astype(jnp.float32))
    return sums, turn_cards, (each - 2) // 2


def showdown_all(payload, tops, ranks, live, cards, out, dense, wide):
    sums, turn_cards, actions = board_values(payload, tops, ranks, live, cards, wide)
    width = sums[0].shape[1]
    flops = sums[0]
    for part in sums[1:]:
        flops += part
    slot = lax.broadcasted_iota(jnp.int32, (SLOTS, 128), 0)
    hits = [(slot.astype(jnp.float32) == card).astype(jnp.float32) for card in turn_cards]
    flop = (slot == TURNS).astype(jnp.float32)
    for a in range(actions):
        for half in range(width // 128):
            lanes = slice(half * 128, half * 128 + 128)
            block = flop * flops[actions + a : actions + a + 1, lanes]
            for hit, part in zip(hits, sums):
                block += hit * part[a : a + 1, lanes]
            column = a * (width // 128) + half
            for tile in range(SLOTS // 8):
                dense[pl.ds(place(column, tile), 8), :] = block[tile * 8 : tile * 8 + 8]
    spots = {place(c, t) for c in range(actions * (width // 128)) for t in range(SLOTS // 8)}
    for spot in sorted(set(range(0, UNITS * 8, 8)) - spots):
        dense[pl.ds(spot, 8), :] = jnp.zeros((8, 128), jnp.float32)
    for k in range(PLANE):
        out[k] = pack(dense[pl.ds(k * CHUNK, CHUNK), :])


def showdown(payload, tops, ranks, live, cards, out, rows, wide):
    sums, turn_cards, actions = board_values(payload, tops, ranks, live, cards, wide)
    halves = sums[0].shape[1] // 128
    flops = sums[0]
    for part in sums[1:]:
        flops += part
    rows[...] = jnp.zeros_like(rows)
    for b, part in enumerate(sums):
        for half in range(halves):
            lanes = slice(half * 128, half * 128 + 128)
            rows[pl.ds((b * halves + half) * actions, actions), :] = part[:actions, lanes]
    for half in range(halves):
        lanes = slice(half * 128, half * 128 + 128)
        at = (len(sums) * halves + half) * actions
        rows[pl.ds(at, actions), :] = flops[actions : 2 * actions, lanes]
    x = rows[...]
    row = lax.broadcasted_iota(jnp.int32, x.shape, 0)
    lane = lax.broadcasted_iota(jnp.int32, x.shape, 1)
    codes, log = encode(x)
    logs = jnp.sum(jnp.where(row == lane, log, 0.0), axis=0, keepdims=True)
    ids = jnp.zeros((1, 128), jnp.float32)
    for b, card in enumerate(turn_cards):
        ids = jnp.where(lane[:1] == b, card, ids)
    codes = jnp.where(row == BOARD_SCALES, logs, codes)
    codes = jnp.where(row == BOARD_SCALES + 1, ids, codes)
    codes = codes.astype(jnp.int32).astype(jnp.int16)
    for k in range(out.shape[0]):
        out[k] = codes


def run_sums(past, blocks, out, rows, page):
    count = blocks.shape[0]
    boards, halves, actions = 4, 2, 9
    tails = [blocks[k, 80:96, :].astype(jnp.int32).astype(jnp.float32) for k in range(count)]
    at = BOARD_SCALES - 80
    logs = jnp.concatenate([tail[at : at + 1] for tail in tails], axis=0)
    scales = jnp.transpose(jnp.exp2(logs * (1.0 / 256.0)) * (1.0 / STEPS))
    for k in range(count):
        codes = blocks[k].astype(jnp.int32).astype(jnp.float32)
        rows[k] = codes * scales[:96, k : k + 1]
    ids = [tail[at + 1 : at + 2] for tail in tails]
    least = ids[0][:, 0:1]
    most = ids[-1][:, boards - 1 : boards]
    slot = lax.broadcasted_iota(jnp.int32, (PAGE, 128), 0).astype(jnp.float32)
    hits = [
        [(slot + past == ids[k][:, b : b + 1] - least).astype(jnp.float32) for b in range(boards)]
        for k in range(count)
    ]
    page[...] = jnp.zeros_like(page)
    for a in range(actions):
        for half in range(halves):
            block = jnp.zeros((PAGE, 128), jnp.float32)
            for k in range(count):
                for b in range(boards):
                    block += hits[k][b] * rows[k, pl.ds((b * halves + half) * actions + a, 1), :]
            page[pl.ds((a * halves + half) * PAGE, PAGE), :] = block
    top, flops = boards * halves * actions, halves * actions
    total = rows[0, pl.ds(top, flops), :]
    for k in range(1, count):
        total += rows[k, pl.ds(top, flops), :]
    page[pl.ds(FLOPS, flops), :] = total
    x = page[...]
    row = lax.broadcasted_iota(jnp.int32, x.shape, 0)
    lane = lax.broadcasted_iota(jnp.int32, x.shape, 1)
    codes, log = encode(x)
    for part in range(2):
        logs = jnp.sum(jnp.where(row == lane + 128 * part, log, 0.0), axis=0, keepdims=True)
        codes = jnp.where(row == PAGE_SCALES + part, logs, codes)
    codes = jnp.where(row == PAGE_SCALES + 2, least, codes)
    codes = jnp.where(row == PAGE_SCALES + 3, most - least + 1.0, codes)
    codes = codes.astype(jnp.int32).astype(jnp.int16)
    for k in range(out.shape[0]):
        out[k] = codes


def finish(turns_over_boards, over_boards, pages, *refs):
    turn_regret, flop_regret, turn_out, flop_out, values, cards, dense = refs[pages:]
    actions, turns, width = turn_regret.shape
    halves, count = width // 128, refs[0].shape[0]
    at = PAGE_SCALES - 160
    dense[...] = jnp.zeros_like(dense)
    flops = jnp.zeros((32, 128), jnp.float32)
    for page, blocks in enumerate(refs[:pages]):
        tails = [blocks[k, 160:176, :].astype(jnp.int32).astype(jnp.float32) for k in range(count)]
        scales = [
            jnp.transpose(
                jnp.exp2(jnp.concatenate([tail[at + part : at + part + 1] for tail in tails], axis=0) * (1.0 / 256.0))
                * (1.0 / STEPS)
            )
            for part in range(2)
        ]
        if page == 0:
            held = jnp.concatenate([tail[at + 3 : at + 4] for tail in tails], axis=0)
            cards[0] = jnp.max(held).astype(jnp.int32)
        leasts = [jnp.max(tail[at + 2 : at + 3]).astype(jnp.int32) for tail in tails]
        for k in range(count):
            codes = blocks[k].astype(jnp.int32).astype(jnp.float32)
            early = codes[:128] * scales[0][:, k : k + 1]
            late = codes[128:] * scales[1][:48, k : k + 1]
            if page == 0:
                flops += late[16:48]
            for column in range(actions * halves):
                start = column * PAGE
                tile = early[start : start + PAGE] if start < 128 else late[start - 128 : start - 128 + PAGE]
                dense[pl.ds(column * SPAN + page * PAGE + leasts[k], PAGE), :] += tile
    for half in range(halves):
        lanes = pl.ds(half * 128, 128)
        weighted = jnp.zeros((turns, 128), jnp.float32)
        weight = jnp.zeros((turns, 128), jnp.float32)
        for a in range(actions):
            q = dense[pl.ds((a * halves + half) * SPAN, turns), :] * turns_over_boards
            regret = turn_regret[a, :, lanes]
            weighted += regret * q
            weight += regret
        value = weighted / weight
        values[:, lanes] = value
        early = flop_regret[:, lanes]
        flop_q = flops[half * actions : half * actions + actions] * over_boards
        root = jnp.sum(early * flop_q, axis=0, keepdims=True) / jnp.sum(early, axis=0, keepdims=True)
        flop_out[:, lanes] = jnp.maximum(early + flop_q - root, 0.0)
        for a in range(actions):
            q = dense[pl.ds((a * halves + half) * SPAN, turns), :] * turns_over_boards
            turn_out[a, :, lanes] = jnp.maximum(turn_regret[a, :, lanes] + q - value, 0.0)


def add_up(blocks, out):
    total = jnp.zeros((CHUNK, 128), jnp.float32)
    for block in unpack(blocks):
        total += block
    row = lax.broadcasted_iota(jnp.int32, total.shape, 0)
    codes = pack(jnp.where(row == SCALES, 0.0, total))
    for k in range(out.shape[0]):
        out[k] = codes


def settle(turns_over_boards, over_boards, blocks, turn_regret, flop_regret, turn_out, flop_out, values, sums):
    actions, turns, width = turn_regret.shape
    halves = width // 128
    for k, block in enumerate(unpack(blocks)):
        sums[pl.ds(k * CHUNK, CHUNK), :] = block

    def column(at):
        tiles = [sums[pl.ds(place(at, tile), 8), :] for tile in range(SLOTS // 8)]
        whole = jnp.concatenate(tiles, axis=0)
        return whole[:turns] * turns_over_boards, whole[turns : turns + 1] * over_boards

    for half in range(halves):
        lanes = pl.ds(half * 128, 128)
        weighted = jnp.zeros((turns, 128), jnp.float32)
        weight = jnp.zeros((turns, 128), jnp.float32)
        top = jnp.zeros((1, 128), jnp.float32)
        bottom = jnp.zeros((1, 128), jnp.float32)
        for a in range(actions):
            q, flop_q = column(a * halves + half)
            regret = turn_regret[a, :, lanes]
            weighted += regret * q
            weight += regret
            early = flop_regret[a : a + 1, lanes]
            top += early * flop_q
            bottom += early
        value = weighted / weight
        values[:, lanes] = value
        root = top / bottom
        for a in range(actions):
            q, flop_q = column(a * halves + half)
            turn_out[a, :, lanes] = jnp.maximum(turn_regret[a, :, lanes] + q - value, 0.0)
            early = flop_regret[a : a + 1, lanes]
            flop_out[a : a + 1, lanes] = jnp.maximum(early + flop_q - root, 0.0)


def shards(
    reach, ranks, live, turn_of, hand_cards, pot, turn_act, flop_act, turn_regret, flop_regret
):
    boards, seqs, width = reach.shape
    total_hands = hand_cards.shape[1]
    turns, actions, _ = turn_regret.shape
    rows = 2 * actions * boards
    boards_all = boards * lax.axis_size("turn")
    params = pltpu.CompilerParams(vmem_limit_bytes=VMEM)
    f32 = jnp.float32

    acts = tuple(x.reshape(1, seqs) for x in (pot, turn_act, flop_act))
    operands = (pot, turn_act, flop_act, turn_of, jnp.transpose(reach, (1, 0, 2)), ranks, live) + acts
    payload, tops = pl.pallas_call(
        weigh,
        out_shape=(
            jax.ShapeDtypeStruct((width // 128, rows + 2 * boards, 128), jnp.int16),
            jax.ShapeDtypeStruct((24, 128), f32),
        ),
        in_specs=[pl.BlockSpec(memory_space=pltpu.HBM)] * 10,
        out_specs=tuple(spread(2)),
        scratch_shapes=[
            pltpu.SMEM(pot.shape, f32),
            pltpu.SMEM(turn_act.shape, jnp.int32),
            pltpu.SMEM(flop_act.shape, jnp.int32),
            pltpu.SMEM(turn_of.shape, jnp.int32),
            pltpu.VMEM((seqs, boards, width), reach.dtype),
            pltpu.VMEM(ranks.shape, jnp.int32),
            pltpu.VMEM(live.shape, jnp.int32),
            *[pltpu.VMEM((1, seqs), x.dtype) for x in acts],
            pltpu.VMEM((width // 128, rows + 2 * boards, 128), f32),
            pltpu.SemaphoreType.DMA((10,)),
            *[pltpu.VMEM((actions, boards, width), f32)] * (2 * BANKS),
        ],
        compiler_params=params,
    )(*[pltpu.with_memory_space_constraint(x, pltpu.HBM) for x in operands])

    gathered = lax.all_gather(payload, "hand", axis=0, tiled=False)

    planes = [[k * LINE + z for k in range(PLANE)] for z in range(LINE)]
    lines = [[k * LINE + z for z in range(LINE)] for k in range(PLANE)]
    vmem = pl.BlockSpec(memory_space=pltpu.VMEM)
    factors = (turns / boards_all / total_hands, 1.0 / boards_all / total_hands)
    by_action = jnp.transpose(turn_regret, (1, 0, 2))
    outputs = (
        jax.ShapeDtypeStruct((actions, turns, width), f32),
        jax.ShapeDtypeStruct((actions, width), f32),
        jax.ShapeDtypeStruct((turns, width), f32),
    )

    def call(kernel, shape, scratch, *args):
        return pl.pallas_call(
            kernel,
            out_shape=jax.ShapeDtypeStruct(shape, jnp.int16),
            in_specs=spread(len(args)),
            out_specs=vmem,
            scratch_shapes=[pltpu.VMEM(dims, f32) for dims in scratch],
            compiler_params=params,
        )(*args)

    def swap(blocks, groups):
        return lax.all_to_all(blocks, "turn", 0, 0, axis_index_groups=groups, tiled=True)

    blocks = call(
        showdown, (LINE, BOARD_ROWS, 128), [(BOARD_ROWS, 128), gathered.shape],
        gathered, tops, ranks, live, hand_cards
    )
    blocks = swap(blocks, lines)
    def page_of(past, boards_of_run):
        shape, scratch = (PLANE, PAGE_ROWS, 128), [(LINE, BOARD_ROWS, 128), (PAGE_ROWS, 128)]
        return swap(call(lambda *refs: run_sums(past, *refs), shape, scratch, boards_of_run), planes)

    def results_of(*pages):
        return pl.pallas_call(
            lambda *refs: finish(*factors, len(pages), *refs),
            out_shape=outputs + (jax.ShapeDtypeStruct((1,), jnp.int32),),
            in_specs=spread(len(pages) + 2),
            out_specs=tuple(spread(3)) + (pl.BlockSpec(memory_space=pltpu.SMEM),),
            scratch_shapes=[pltpu.VMEM((actions * (width // 128) * SPAN, 128), f32)],
            compiler_params=params,
        )(*pages, by_action, flop_regret)

    page = page_of(0.0, blocks)
    turn_out, flop_out, values, cards = results_of(page)

    def next_page(state):
        again = blocks + jnp.where(state[0] > PAGE, 0, 1).astype(jnp.int16)
        *results, held = results_of(page, page_of(float(PAGE), again))
        state = lax.while_loop(lambda s: s[0] > 2 * PAGE, every_card, (held[0], *results))
        return (jnp.int32(0),) + tuple(state[1:])

    def every_card(state):
        payload = gathered + jnp.where(state[0] > 2 * PAGE, 0, 1).astype(jnp.int16)
        scratch = [(UNITS * 8, 128), gathered.shape]
        chunks = call(
            showdown_all, (PLANE, CHUNK, 128), scratch, payload, tops, ranks, live, hand_cards
        )
        chunks = swap(chunks, planes)
        chunks = swap(call(add_up, (LINE, CHUNK, 128), [], chunks), lines)
        chunks = swap(call(add_up, (PLANE, CHUNK, 128), [], chunks), planes)
        results = pl.pallas_call(
            lambda *refs: settle(*factors, *refs),
            out_shape=outputs,
            in_specs=spread(3),
            out_specs=tuple(spread(3)),
            scratch_shapes=[pltpu.VMEM((UNITS * 8, 128), f32)],
            compiler_params=params,
        )(chunks, by_action, flop_regret)
        return (jnp.int32(0),) + tuple(results)

    state = (cards[0], turn_out, flop_out, values)
    _, turn_out, flop_out, values = lax.while_loop(lambda s: s[0] > PAGE, next_page, state)
    return (jnp.transpose(turn_out, (1, 0, 2)), flop_out, values)


def solution(mesh):
    return jax.shard_map(
        shards,
        mesh=mesh,
        in_specs=(
            P("turn", None, "hand"),
            P("turn", "hand"),
            P("turn", "hand"),
            P("turn"),
            P(),
            P(),
            P(),
            P(),
            P(None, None, "hand"),
            P(None, "hand"),
        ),
        out_specs=(P(None, None, "hand"), P(None, "hand"), P(None, "hand")),
        check_vma=False,
    )
```

```python
import jax
import jax.numpy as jnp
from jax import lax
from jax.experimental import pallas as pl
from jax.experimental.pallas import tpu as pltpu
from jax.sharding import PartitionSpec as P

TURNS = 49
SLOTS = 56
UNITS = 128
PLANE = 16
LINE = 8
CHUNK = UNITS * 8 // PLANE
STEPS = 32760.0
SCALES = 58
BOARD_ROWS = 96
BOARD_SCALES = 90
PAGE = 8
FLOPS = 144
PAGE_SCALES = 162
PAGE_ROWS = 176
SPAN = 64
VMEM = 48 * 1024 * 1024
BANKS = 4


def spread(count):
    return [pl.BlockSpec(memory_space=pltpu.VMEM)] * count


def place(column, tile):
    columns, tiles = UNITS // (SLOTS // 8), SLOTS // 8
    if tile == tiles - 1 and column < PLANE:
        return column * CHUNK + CHUNK - 8
    spot = column * (tiles - 1) + tile if tile < tiles - 1 else columns * (tiles - 1) + column - PLANE
    return spot // 7 * CHUNK + spot % 7 * 8


def encode(x):
    top = jnp.maximum(jnp.max(jnp.abs(x), axis=1, keepdims=True), 1e-30)
    log = jnp.ceil(jnp.log2(top) * 256.0)
    return jnp.round(x * (STEPS / jnp.exp2(log * (1.0 / 256.0)))), log


def pack(x):
    row = lax.broadcasted_iota(jnp.int32, x.shape, 0)
    lane = lax.broadcasted_iota(jnp.int32, x.shape, 1)
    codes, log = encode(x)
    logs = jnp.sum(jnp.where(row == lane, log, 0.0), axis=0, keepdims=True)
    return jnp.where(row == SCALES, logs, codes).astype(jnp.int32).astype(jnp.int16)


def unpack(blocks):
    count = blocks.shape[0]
    ends = [blocks[k, 48:64, :].astype(jnp.int32).astype(jnp.float32) for k in range(count)]
    logs = jnp.concatenate([end[SCALES - 48 : SCALES - 47] for end in ends], axis=0)
    scales = jnp.transpose(jnp.exp2(logs * (1.0 / 256.0)) * (1.0 / STEPS))
    for k in range(count):
        codes = blocks[k].astype(jnp.int32).astype(jnp.float32)
        yield codes * scales[:64, k : k + 1]


def row_tops(pot, turn_act, flop_act, count):
    row = lax.broadcasted_iota(jnp.int32, (24, pot.shape[1]), 0)
    key = jnp.where(row < count, turn_act[...], flop_act[...] + count)
    return jnp.sum(jnp.where(row == key, pot[...], 0.0), axis=1, keepdims=True)


def weigh(
    pot_hbm, turn_hbm, flop_hbm, of_hbm, reach_hbm, ranks_hbm, live_hbm, pots_hbm, turns_hbm, flops_hbm, out, tops,
    pot, turn_act, flop_act, turn_of, reach, ranks, live, pots, turns, flops, stage, sems, *banks
):
    pairs = (
        (reach_hbm, reach), (pot_hbm, pot), (turn_hbm, turn_act), (flop_hbm, flop_act),
        (of_hbm, turn_of), (ranks_hbm, ranks), (live_hbm, live),
        (pots_hbm, pots), (turns_hbm, turns), (flops_hbm, flops),
    )
    moves = [pltpu.make_async_copy(x, y, sems.at[k]) for k, (x, y) in enumerate(pairs)]
    for move in moves:
        move.start()
    turn_sums, flop_sums = banks[:BANKS], banks[BANKS:]
    for bank in banks:
        bank[...] = jnp.zeros_like(bank)
    for move in moves:
        move.wait()
    seqs, boards, width = reach.shape
    halves = [slice(half * 128, half * 128 + 128) for half in range(width // 128)]
    for s in range(seqs):
        term = reach[s].astype(jnp.float32) * pot[s]
        turn_sums[s % BANKS][turn_act[s]] += term
        flop_sums[s % BANKS][flop_act[s]] += term
    alive = live[...].astype(jnp.float32)
    most = row_tops(pots, turns, flops, turn_sums[0].shape[0])
    tops[...] = jnp.broadcast_to(most, tops.shape)
    steps = 65535.0 / jnp.maximum(most, 1e-30)
    top = 0
    for sums in (turn_sums, flop_sums):
        for r in range(sums[0].shape[0]):
            total = sums[0][r]
            for other in sums[1:]:
                total += other[r]
            at = top // boards
            total = jnp.round(total * alive * steps[at : at + 1])
            total = jnp.minimum(total, 65535.0) - 32768.0
            for half, lanes in enumerate(halves):
                stage[half, pl.ds(top, boards), :] = total[:, lanes]
            top += boards
    for half, lanes in enumerate(halves):
        stage[half, pl.ds(top, boards), :] = ranks[:, lanes].astype(jnp.float32)
        for b in range(boards):
            card = jnp.full((1, 128), turn_of[b], jnp.int32).astype(jnp.float32)
            stage[half, pl.ds(top + boards + b, 1), :] = card
    out[...] = stage[...].astype(jnp.int32).astype(jnp.int16)


def board_values(payload, tops, ranks, live, cards, wide):
    hands, halves, rows, _ = payload.shape
    width = halves * 128
    boards = ranks.shape[0]
    each = rows // boards
    me = lax.axis_index("hand")
    here = cards[:, pl.ds(pl.multiple_of(me * width, width), width)].astype(jnp.float32)
    mine = jnp.concatenate(
        [ranks[...].astype(jnp.float32), here, jnp.zeros((2, width), jnp.float32)], axis=0
    )
    columns = jnp.transpose(mine)
    first, second = columns[:, boards : boards + 1], columns[:, boards + 1 : boards + 2]
    aparts = []
    for h in range(hands):
        there = cards[:, h * width : (h + 1) * width].astype(jnp.float32)
        one, two = there[0:1], there[1:2]
        shared = (first == one) | (first == two) | (second == one) | (second == two)
        aparts.append(jnp.where(shared, 0.0, 1.0))
    apart = jnp.concatenate(aparts, axis=1)
    tall = -(-each // 8) * 8
    wide[...] = payload[...].astype(jnp.int32).astype(jnp.float32)
    unit = tops[:, 0:1] * (1.0 / 65535.0)
    sums, turn_cards = [], []
    for b in range(boards):
        x = jnp.concatenate(
            [wide[h, half, pl.ds(b, each, stride=boards), :] for h in range(hands) for half in range(halves)],
            axis=1,
        )
        theirs = x[each - 2 : each - 1]
        turn_cards.append(x[each - 1 : each, :128])
        x = jnp.concatenate([x, jnp.zeros((tall - each, hands * width), jnp.float32)], axis=0)
        x += 32768.0
        high = jnp.floor(x * (1.0 / 256.0))
        pieces = jnp.concatenate([high, x - high * 256.0], axis=0).astype(jnp.bfloat16)
        sign = jnp.clip(columns[:, b : b + 1] - theirs, -1.0, 1.0)
        tile = (sign * apart).astype(jnp.bfloat16)
        part = lax.dot_general(
            pieces, tile, (((1,), (1,)), ((), ())), preferred_element_type=jnp.float32
        )
        part = (part[:tall] * 256.0 + part[tall:]) * unit
        sums.append(part * live[b : b + 1, :].astype(jnp.float32))
    return sums, turn_cards, (each - 2) // 2


def showdown_all(payload, tops, ranks, live, cards, out, dense, wide):
    sums, turn_cards, actions = board_values(payload, tops, ranks, live, cards, wide)
    width = sums[0].shape[1]
    flops = sums[0]
    for part in sums[1:]:
        flops += part
    slot = lax.broadcasted_iota(jnp.int32, (SLOTS, 128), 0)
    hits = [(slot.astype(jnp.float32) == card).astype(jnp.float32) for card in turn_cards]
    flop = (slot == TURNS).astype(jnp.float32)
    for a in range(actions):
        for half in range(width // 128):
            lanes = slice(half * 128, half * 128 + 128)
            block = flop * flops[actions + a : actions + a + 1, lanes]
            for hit, part in zip(hits, sums):
                block += hit * part[a : a + 1, lanes]
            column = a * (width // 128) + half
            for tile in range(SLOTS // 8):
                dense[pl.ds(place(column, tile), 8), :] = block[tile * 8 : tile * 8 + 8]
    spots = {place(c, t) for c in range(actions * (width // 128)) for t in range(SLOTS // 8)}
    for spot in sorted(set(range(0, UNITS * 8, 8)) - spots):
        dense[pl.ds(spot, 8), :] = jnp.zeros((8, 128), jnp.float32)
    for k in range(PLANE):
        out[k] = pack(dense[pl.ds(k * CHUNK, CHUNK), :])


def showdown(payload, tops, ranks, live, cards, out, rows, wide):
    sums, turn_cards, actions = board_values(payload, tops, ranks, live, cards, wide)
    halves = sums[0].shape[1] // 128
    flops = sums[0]
    for part in sums[1:]:
        flops += part
    rows[...] = jnp.zeros_like(rows)
    for b, part in enumerate(sums):
        for half in range(halves):
            lanes = slice(half * 128, half * 128 + 128)
            rows[pl.ds((b * halves + half) * actions, actions), :] = part[:actions, lanes]
    for half in range(halves):
        lanes = slice(half * 128, half * 128 + 128)
        at = (len(sums) * halves + half) * actions
        rows[pl.ds(at, actions), :] = flops[actions : 2 * actions, lanes]
    x = rows[...]
    row = lax.broadcasted_iota(jnp.int32, x.shape, 0)
    lane = lax.broadcasted_iota(jnp.int32, x.shape, 1)
    codes, log = encode(x)
    logs = jnp.sum(jnp.where(row == lane, log, 0.0), axis=0, keepdims=True)
    ids = jnp.zeros((1, 128), jnp.float32)
    for b, card in enumerate(turn_cards):
        ids = jnp.where(lane[:1] == b, card, ids)
    codes = jnp.where(row == BOARD_SCALES, logs, codes)
    codes = jnp.where(row == BOARD_SCALES + 1, ids, codes)
    codes = codes.astype(jnp.int32).astype(jnp.int16)
    for k in range(out.shape[0]):
        out[k] = codes


def run_sums(past, blocks, out, rows, page):
    count = blocks.shape[0]
    boards, halves, actions = 4, 2, 9
    tails = [blocks[k, 80:96, :].astype(jnp.int32).astype(jnp.float32) for k in range(count)]
    at = BOARD_SCALES - 80
    logs = jnp.concatenate([tail[at : at + 1] for tail in tails], axis=0)
    scales = jnp.transpose(jnp.exp2(logs * (1.0 / 256.0)) * (1.0 / STEPS))
    for k in range(count):
        codes = blocks[k].astype(jnp.int32).astype(jnp.float32)
        rows[k] = codes * scales[:96, k : k + 1]
    ids = [tail[at + 1 : at + 2] for tail in tails]
    least = ids[0][:, 0:1]
    most = ids[-1][:, boards - 1 : boards]
    slot = lax.broadcasted_iota(jnp.int32, (PAGE, 128), 0).astype(jnp.float32)
    hits = [
        [(slot + past == ids[k][:, b : b + 1] - least).astype(jnp.float32) for b in range(boards)]
        for k in range(count)
    ]
    page[...] = jnp.zeros_like(page)
    for a in range(actions):
        for half in range(halves):
            block = jnp.zeros((PAGE, 128), jnp.float32)
            for k in range(count):
                for b in range(boards):
                    block += hits[k][b] * rows[k, pl.ds((b * halves + half) * actions + a, 1), :]
            page[pl.ds((a * halves + half) * PAGE, PAGE), :] = block
    top, flops = boards * halves * actions, halves * actions
    total = rows[0, pl.ds(top, flops), :]
    for k in range(1, count):
        total += rows[k, pl.ds(top, flops), :]
    page[pl.ds(FLOPS, flops), :] = total
    x = page[...]
    row = lax.broadcasted_iota(jnp.int32, x.shape, 0)
    lane = lax.broadcasted_iota(jnp.int32, x.shape, 1)
    codes, log = encode(x)
    for part in range(2):
        logs = jnp.sum(jnp.where(row == lane + 128 * part, log, 0.0), axis=0, keepdims=True)
        codes = jnp.where(row == PAGE_SCALES + part, logs, codes)
    codes = jnp.where(row == PAGE_SCALES + 2, least, codes)
    codes = jnp.where(row == PAGE_SCALES + 3, most - least + 1.0, codes)
    codes = codes.astype(jnp.int32).astype(jnp.int16)
    for k in range(out.shape[0]):
        out[k] = codes


def finish(turns_over_boards, over_boards, pages, *refs):
    turn_regret, flop_regret, turn_out, flop_out, values, cards, dense = refs[pages:]
    actions, turns, width = turn_regret.shape
    halves, count = width // 128, refs[0].shape[0]
    at = PAGE_SCALES - 160
    dense[...] = jnp.zeros_like(dense)
    flops = jnp.zeros((32, 128), jnp.float32)
    for page, blocks in enumerate(refs[:pages]):
        tails = [blocks[k, 160:176, :].astype(jnp.int32).astype(jnp.float32) for k in range(count)]
        scales = [
            jnp.transpose(
                jnp.exp2(jnp.concatenate([tail[at + part : at + part + 1] for tail in tails], axis=0) * (1.0 / 256.0))
                * (1.0 / STEPS)
            )
            for part in range(2)
        ]
        if page == 0:
            held = jnp.concatenate([tail[at + 3 : at + 4] for tail in tails], axis=0)
            cards[0] = jnp.max(held).astype(jnp.int32)
        leasts = [jnp.max(tail[at + 2 : at + 3]).astype(jnp.int32) for tail in tails]
        for k in range(count):
            codes = blocks[k].astype(jnp.int32).astype(jnp.float32)
            early = codes[:128] * scales[0][:, k : k + 1]
            late = codes[128:] * scales[1][:48, k : k + 1]
            if page == 0:
                flops += late[16:48]
            for column in range(actions * halves):
                start = column * PAGE
                tile = early[start : start + PAGE] if start < 128 else late[start - 128 : start - 128 + PAGE]
                dense[pl.ds(column * SPAN + page * PAGE + leasts[k], PAGE), :] += tile
    for half in range(halves):
        lanes = pl.ds(half * 128, 128)
        weighted = jnp.zeros((turns, 128), jnp.float32)
        weight = jnp.zeros((turns, 128), jnp.float32)
        for a in range(actions):
            q = dense[pl.ds((a * halves + half) * SPAN, turns), :] * turns_over_boards
            regret = turn_regret[a, :, lanes]
            weighted += regret * q
            weight += regret
        value = weighted / weight
        values[:, lanes] = value
        early = flop_regret[:, lanes]
        flop_q = flops[half * actions : half * actions + actions] * over_boards
        root = jnp.sum(early * flop_q, axis=0, keepdims=True) / jnp.sum(early, axis=0, keepdims=True)
        flop_out[:, lanes] = jnp.maximum(early + flop_q - root, 0.0)
        for a in range(actions):
            q = dense[pl.ds((a * halves + half) * SPAN, turns), :] * turns_over_boards
            turn_out[a, :, lanes] = jnp.maximum(turn_regret[a, :, lanes] + q - value, 0.0)


def add_up(blocks, out):
    total = jnp.zeros((CHUNK, 128), jnp.float32)
    for block in unpack(blocks):
        total += block
    row = lax.broadcasted_iota(jnp.int32, total.shape, 0)
    codes = pack(jnp.where(row == SCALES, 0.0, total))
    for k in range(out.shape[0]):
        out[k] = codes


def settle(turns_over_boards, over_boards, blocks, turn_regret, flop_regret, turn_out, flop_out, values, sums):
    actions, turns, width = turn_regret.shape
    halves = width // 128
    for k, block in enumerate(unpack(blocks)):
        sums[pl.ds(k * CHUNK, CHUNK), :] = block

    def column(at):
        tiles = [sums[pl.ds(place(at, tile), 8), :] for tile in range(SLOTS // 8)]
        whole = jnp.concatenate(tiles, axis=0)
        return whole[:turns] * turns_over_boards, whole[turns : turns + 1] * over_boards

    for half in range(halves):
        lanes = pl.ds(half * 128, 128)
        weighted = jnp.zeros((turns, 128), jnp.float32)
        weight = jnp.zeros((turns, 128), jnp.float32)
        top = jnp.zeros((1, 128), jnp.float32)
        bottom = jnp.zeros((1, 128), jnp.float32)
        for a in range(actions):
            q, flop_q = column(a * halves + half)
            regret = turn_regret[a, :, lanes]
            weighted += regret * q
            weight += regret
            early = flop_regret[a : a + 1, lanes]
            top += early * flop_q
            bottom += early
        value = weighted / weight
        values[:, lanes] = value
        root = top / bottom
        for a in range(actions):
            q, flop_q = column(a * halves + half)
            turn_out[a, :, lanes] = jnp.maximum(turn_regret[a, :, lanes] + q - value, 0.0)
            early = flop_regret[a : a + 1, lanes]
            flop_out[a : a + 1, lanes] = jnp.maximum(early + flop_q - root, 0.0)


def shards(
    reach, ranks, live, turn_of, hand_cards, pot, turn_act, flop_act, turn_regret, flop_regret
):
    boards, seqs, width = reach.shape
    total_hands = hand_cards.shape[1]
    turns, actions, _ = turn_regret.shape
    rows = 2 * actions * boards
    boards_all = boards * lax.axis_size("turn")
    params = pltpu.CompilerParams(vmem_limit_bytes=VMEM)
    f32 = jnp.float32

    acts = tuple(x.reshape(1, seqs) for x in (pot, turn_act, flop_act))
    operands = (pot, turn_act, flop_act, turn_of, jnp.transpose(reach, (1, 0, 2)), ranks, live) + acts
    payload, tops = pl.pallas_call(
        weigh,
        out_shape=(
            jax.ShapeDtypeStruct((width // 128, rows + 2 * boards, 128), jnp.int16),
            jax.ShapeDtypeStruct((24, 128), f32),
        ),
        in_specs=[pl.BlockSpec(memory_space=pltpu.HBM)] * 10,
        out_specs=tuple(spread(2)),
        scratch_shapes=[
            pltpu.SMEM(pot.shape, f32),
            pltpu.SMEM(turn_act.shape, jnp.int32),
            pltpu.SMEM(flop_act.shape, jnp.int32),
            pltpu.SMEM(turn_of.shape, jnp.int32),
            pltpu.VMEM((seqs, boards, width), reach.dtype),
            pltpu.VMEM(ranks.shape, jnp.int32),
            pltpu.VMEM(live.shape, jnp.int32),
            *[pltpu.VMEM((1, seqs), x.dtype) for x in acts],
            pltpu.VMEM((width // 128, rows + 2 * boards, 128), f32),
            pltpu.SemaphoreType.DMA((10,)),
            *[pltpu.VMEM((actions, boards, width), f32)] * (2 * BANKS),
        ],
        compiler_params=params,
    )(*[pltpu.with_memory_space_constraint(x, pltpu.HBM) for x in operands])

    gathered = lax.all_gather(payload, "hand", axis=0, tiled=False)

    planes = [[k * LINE + z for k in range(PLANE)] for z in range(LINE)]
    lines = [[k * LINE + z for z in range(LINE)] for k in range(PLANE)]
    vmem = pl.BlockSpec(memory_space=pltpu.VMEM)
    factors = (turns / boards_all / total_hands, 1.0 / boards_all / total_hands)
    by_action = jnp.transpose(turn_regret, (1, 0, 2))
    outputs = (
        jax.ShapeDtypeStruct((actions, turns, width), f32),
        jax.ShapeDtypeStruct((actions, width), f32),
        jax.ShapeDtypeStruct((turns, width), f32),
    )

    def call(kernel, shape, scratch, *args):
        return pl.pallas_call(
            kernel,
            out_shape=jax.ShapeDtypeStruct(shape, jnp.int16),
            in_specs=spread(len(args)),
            out_specs=vmem,
            scratch_shapes=[pltpu.VMEM(dims, f32) for dims in scratch],
            compiler_params=params,
        )(*args)

    def swap(blocks, groups):
        return lax.all_to_all(blocks, "turn", 0, 0, axis_index_groups=groups, tiled=True)

    blocks = call(
        showdown, (LINE, BOARD_ROWS, 128), [(BOARD_ROWS, 128), gathered.shape],
        gathered, tops, ranks, live, hand_cards
    )
    blocks = swap(blocks, lines)
    def page_of(past, boards_of_run):
        shape, scratch = (PLANE, PAGE_ROWS, 128), [(LINE, BOARD_ROWS, 128), (PAGE_ROWS, 128)]
        return swap(call(lambda *refs: run_sums(past, *refs), shape, scratch, boards_of_run), planes)

    def results_of(*pages):
        return pl.pallas_call(
            lambda *refs: finish(*factors, len(pages), *refs),
            out_shape=outputs + (jax.ShapeDtypeStruct((1,), jnp.int32),),
            in_specs=spread(len(pages) + 2),
            out_specs=tuple(spread(3)) + (pl.BlockSpec(memory_space=pltpu.SMEM),),
            scratch_shapes=[pltpu.VMEM((actions * (width // 128) * SPAN, 128), f32)],
            compiler_params=params,
        )(*pages, by_action, flop_regret)

    page = page_of(0.0, blocks)
    turn_out, flop_out, values, cards = results_of(page)

    def next_page(state):
        again = blocks + jnp.where(state[0] > PAGE, 0, 1).astype(jnp.int16)
        *results, held = results_of(page, page_of(float(PAGE), again))
        state = lax.while_loop(lambda s: s[0] > 2 * PAGE, every_card, (held[0], *results))
        return (jnp.int32(0),) + tuple(state[1:])

    def every_card(state):
        payload = gathered + jnp.where(state[0] > 2 * PAGE, 0, 1).astype(jnp.int16)
        scratch = [(UNITS * 8, 128), gathered.shape]
        chunks = call(
            showdown_all, (PLANE, CHUNK, 128), scratch, payload, tops, ranks, live, hand_cards
        )
        chunks = swap(chunks, planes)
        chunks = swap(call(add_up, (LINE, CHUNK, 128), [], chunks), lines)
        chunks = swap(call(add_up, (PLANE, CHUNK, 128), [], chunks), planes)
        results = pl.pallas_call(
            lambda *refs: settle(*factors, *refs),
            out_shape=outputs,
            in_specs=spread(3),
            out_specs=tuple(spread(3)),
            scratch_shapes=[pltpu.VMEM((UNITS * 8, 128), f32)],
            compiler_params=params,
        )(chunks, by_action, flop_regret)
        return (jnp.int32(0),) + tuple(results)

    state = (cards[0], turn_out, flop_out, values)
    _, turn_out, flop_out, values = lax.cond(state[0] > PAGE, next_page, lambda s: s, state)
    return (jnp.transpose(turn_out, (1, 0, 2)), flop_out, values)


def solution(mesh):
    return jax.shard_map(
        shards,
        mesh=mesh,
        in_specs=(
            P("turn", None, "hand"),
            P("turn", "hand"),
            P("turn", "hand"),
            P("turn"),
            P(),
            P(),
            P(),
            P(),
            P(None, None, "hand"),
            P(None, "hand"),
        ),
        out_specs=(P(None, None, "hand"), P(None, "hand"), P(None, "hand")),
        check_vma=False,
    )
```
